32 devices in a mesh: pipe: 4 (over z), expert: 8 (over y, x, core).
Axes of the slice: x: 2, y: 2, z: 4, core: 2. Of those that a mesh axis runs over, the one named last changes fastest.
Arguments:
- enc_states: bfloat16 [32, 512], P('pipe'), may hold values from -6 to 6
- key_weight: bfloat16 [512, 512], P(None, 'expert'), may hold values from -0.25 to 0.25
- value_weight: bfloat16 [512, 512], P(None, 'expert'), may hold values from -0.25 to 0.25
- queries: bfloat16 [4096, 512], P('pipe', 'expert'), may hold values from -240 to 240
- lengths: int32 [4096], P('pipe'), may hold values from 1 to 32
- context_grad: bfloat16 [4096, 512], P('pipe', 'expert'), may hold values from -6 to 6
- residual: bfloat16 [4096, 512], P(('pipe', 'expert')), may hold values from -6 to 6
- norm_gain: bfloat16 [512], replicated, may hold values from 0.5 to 1.5
- routes: int32 [4096, 1], P(('pipe', 'expert')), may hold values from 0 to 7
- w_in: bfloat16 [8, 512, 1280], P('expert', None, 'pipe'), may hold values from -0.25 to 0.25
- w_out: bfloat16 [8, 1280, 512], P('expert', 'pipe'), may hold values from -0.15625 to 0.15625
Outputs:
- layer_out: bfloat16 [4096, 512], P(('pipe', 'expert'))
- enc_grad: bfloat16 [32, 512], P('pipe')
The draws below stay inside these ranges and needn't reach their ends.
All inputs are finite; a program needn't handle non-finite values.
Results may differ from the reference program's by a relative error of at most 0.013.
The reference program's roundings to bfloat16 on the way (of `probs_low`, `context`, `normed`, `active`, `expert_out`, `grad_scores` and `grad_keys`) count: a program that leaves them out, or rounds other values in their place, can miss the bound.
Values may be sent and summed in bfloat16 or wider, within the bound.
No kernel may reach another device: no remote copies, remote signals or barrier semaphores. Data moves between devices by JAX's collectives and lax.ppermute only.
A program may use at most 64 MiB of HBM per device.

```python
import math
import jax
import jax.numpy as jnp
from jax import lax

HEAD = 64
FF_DEV = 320
TOK_DEV = 128
HEADS = 8
D = 512
EXPERTS = 8
FF = 1280
CAP = 8
ENC = 32
TOKENS = 4096
N_PIPE = 4


def draw_queries(key, part):
    key = jax.random.fold_in(key, 11)
    normal_key = jax.random.fold_in(key, 0)
    entries = jnp.clip(jax.random.normal(normal_key, (TOKENS, D), jnp.float32), -6.0, 6.0)
    return entries.astype(jnp.bfloat16)


def plant(values, rng, least, top_value):
    spot = [jax.random.randint(jax.random.fold_in(rng, axis), (), 0, length) for axis, length in enumerate(values.shape)]
    main_axis = values.shape.index(max(values.shape))
    next_to = spot[:main_axis] + [(spot[main_axis] + 1) % values.shape[main_axis]] + spot[main_axis + 1:]
    return values.at[tuple(spot)].set(least).at[tuple(next_to)].set(top_value)


def block_levels(stream_key, shape, cuts, smallest, high):
    loudness = 1.0
    for position, shards_of in cuts:
        steps = jax.random.uniform(jax.random.fold_in(jax.random.fold_in(stream_key, 6), position), (shards_of,), jnp.float32, smallest / len(cuts), high / len(cuts))
        loudness = loudness * jnp.repeat(jnp.exp(steps), shape[position] // shards_of).reshape((-1,) + (1,) * (len(shape) - 1 - position))
    return loudness


def picks_of(own_key, rows, count, top, lift):
    order = jax.random.permutation(jax.random.fold_in(own_key, 1), count)
    pull = order
    for power in range(3):
        pull = pull * pull // count
    pull = pull * lift // count
    lots = jax.random.randint(jax.random.fold_in(own_key, 2), (rows, count), 0, 4096) + pull
    sure = jax.random.permutation(jax.random.fold_in(own_key, 3), rows)[jnp.arange(count) % rows]
    lots = jnp.where(jnp.arange(rows)[:, None] == sure[None, :], 1 << 14, lots)
    merit = lots * count + jnp.arange(count)
    return lax.top_k(merit.astype(jnp.int32), top)[1].astype(jnp.int32)


def gaussian(stream_key, dims, scale, limit, pieces=(), kind=jnp.bfloat16):
    result = scale * jax.random.normal(stream_key, dims, jnp.float32)
    if pieces:
        result = result * block_levels(stream_key, dims, pieces, -0.22, 0.18)
    return jnp.clip(result, -limit, limit).astype(kind)


def setup_inputs(seed: int = 0) -> dict:
    key_list = jax.random.split(jax.random.key(seed), 12)
    return {
        "enc_states": gaussian(key_list[0], (ENC, D), 1.0, 6.0, ((0, 4),)),
        "key_weight": gaussian(key_list[1], (D, D), D ** -0.5, 0.25, ((1, 8),)),
        "value_weight": gaussian(key_list[2], (D, D), D ** -0.5, 0.25, ((1, 8),)),
        "queries": draw_queries(jax.random.fold_in(key_list[11], 71), 0),
        "lengths": plant(jax.random.randint(key_list[4], (TOKENS,), 1, ENC + 1), jax.random.fold_in(key_list[4], 1), 1, ENC).astype(jnp.int32),
        "context_grad": gaussian(key_list[5], (TOKENS, D), 1.0, 6.0, ((0, 4), (1, 8))),
        "residual": gaussian(key_list[6], (TOKENS, D), 1.0, 6.0, ((0, 32),)),
        "norm_gain": jnp.clip(1.0 + 0.1 * jax.random.normal(key_list[7], (D,), jnp.float32), 0.5, 1.5).astype(jnp.bfloat16),
        "routes": picks_of(key_list[8], TOKENS, EXPERTS, 1, 2048),
        "w_in": gaussian(key_list[9], (EXPERTS, D, FF), D ** -0.5, 0.25, ((0, 8), (2, 4))),
        "w_out": gaussian(key_list[10], (EXPERTS, FF, D), FF ** -0.5, 0.15625, ((0, 8), (1, 4))),
    }


def reference(enc_states, key_weight, value_weight, queries, lengths, context_grad, residual, norm_gain, routes, w_in, w_out):
    scale = 1.0 / math.sqrt(HEAD)
    keys = jnp.dot(enc_states, key_weight, preferred_element_type=jnp.float32).astype(jnp.bfloat16)
    values = jnp.dot(enc_states, value_weight, preferred_element_type=jnp.float32).astype(jnp.bfloat16)
    visible = jnp.arange(ENC, dtype=jnp.int32)[None, :] < lengths[:, None]

    def per_head(head_index):
        first = (head_index * HEAD).astype(jnp.int32)
        query = lax.dynamic_slice_in_dim(queries, first, HEAD, 1)
        key_cols = lax.dynamic_slice_in_dim(keys, first, HEAD, 1)
        value_cols = lax.dynamic_slice_in_dim(values, first, HEAD, 1)
        grad_cols = lax.dynamic_slice_in_dim(context_grad, first, HEAD, 1)
        scores = jnp.dot(query, key_cols.T, preferred_element_type=jnp.float32) * scale
        scores = jnp.where(visible, scores, -1e+30)
        highest = lax.optimization_barrier(jnp.max(scores, axis=1, keepdims=True))
        weights = jnp.where(visible, jnp.exp(scores - highest), 0.0)
        probs = weights / lax.optimization_barrier(jnp.sum(weights, axis=1, keepdims=True))
        probs_low = probs.astype(jnp.bfloat16)
        context = jnp.dot(probs_low, value_cols, preferred_element_type=jnp.float32).astype(jnp.bfloat16)
        grad_values = jnp.dot(probs_low.T, grad_cols, preferred_element_type=jnp.float32)
        grad_probs = jnp.dot(grad_cols, value_cols.T, preferred_element_type=jnp.float32)
        row_delta = lax.optimization_barrier(jnp.sum(probs * grad_probs, axis=1, keepdims=True))
        grad_scores = (probs * (grad_probs - row_delta) * scale).astype(jnp.bfloat16)
        grad_keys = jnp.dot(grad_scores.T, query, preferred_element_type=jnp.float32)
        return (context, grad_keys, grad_values)
    contexts, key_grads, value_grads = lax.map(per_head, jnp.arange(HEADS, dtype=jnp.int32))
    context = jnp.transpose(contexts, (1, 0, 2)).reshape(TOKENS, D)
    grad_keys = jnp.transpose(key_grads, (1, 0, 2)).reshape(ENC, D).astype(jnp.bfloat16)
    grad_values = jnp.transpose(value_grads, (1, 0, 2)).reshape(ENC, D).astype(jnp.bfloat16)
    enc_grad = (jnp.dot(grad_keys, key_weight.T, preferred_element_type=jnp.float32) + jnp.dot(grad_values, value_weight.T, preferred_element_type=jnp.float32)).astype(jnp.bfloat16)
    hidden_state = residual.astype(jnp.float32) + context.astype(jnp.float32)
    power = lax.optimization_barrier(jnp.mean(hidden_state * hidden_state, axis=1, keepdims=True))
    normed = (hidden_state * lax.rsqrt(power + 1e-06) * norm_gain.astype(jnp.float32)).astype(jnp.bfloat16)
    blocks = TOKENS // TOK_DEV
    expert_ids = routes[:, 0]
    grouped = expert_ids.reshape(blocks, TOK_DEV)
    onehot = (grouped[:, :, None] == jnp.arange(EXPERTS, dtype=jnp.int32)[None, None, :]).astype(jnp.int32)
    slot_rank = lax.optimization_barrier(jnp.sum((jnp.cumsum(onehot, axis=1) - onehot) * onehot, axis=2))
    kept = slot_rank < CAP
    slot_row = jnp.where(kept, jnp.arange(blocks, dtype=jnp.int32)[:, None] * CAP + slot_rank, blocks * CAP)
    slot_row = slot_row.reshape(TOKENS).astype(jnp.int32)
    buffer = jnp.zeros((EXPERTS, blocks * CAP, D), jnp.bfloat16).at[expert_ids, slot_row].set(normed, mode='drop')

    def per_expert(operands):
        slot_rows, first_weight, second_weight = operands
        active = jnp.maximum(jnp.dot(slot_rows, first_weight, preferred_element_type=jnp.float32), 0.0).astype(jnp.bfloat16)
        grouped_active = active.reshape(slot_rows.shape[0], N_PIPE, FF_DEV).astype(jnp.float32)
        grouped_weight = second_weight.reshape(N_PIPE, FF_DEV, D).astype(jnp.float32)
        parts = jnp.einsum('rpf,pfd->prd', grouped_active, grouped_weight)
        rounded = lax.optimization_barrier(parts.astype(jnp.bfloat16))
        return lax.optimization_barrier(jnp.sum(rounded.astype(jnp.float32), axis=0)).astype(jnp.bfloat16)
    outputs = lax.map(per_expert, (buffer, w_in, w_out))
    expert_out = outputs.at[expert_ids, slot_row].get(mode='fill', fill_value=0).astype(jnp.float32)
    layer_out = (hidden_state + expert_out).astype(jnp.bfloat16)
    return (layer_out, enc_grad)
```

```python
import math

import jax
import jax.numpy as jnp
from jax import lax
from jax.sharding import PartitionSpec as P


def shifted(value, axis, step):
    size = lax.axis_size(axis)
    return lax.ppermute(value, axis, [(i, (i + step) % size) for i in range(size)])


def per_device(
    enc_states,
    key_weight,
    value_weight,
    queries,
    lengths,
    context_grad,
    residual,
    norm_gain,
    routes,
    w_in,
    w_out,
):
    enc_dev = enc_states.shape[0]
    head = key_weight.shape[1]
    tok_dev = residual.shape[0]
    model = residual.shape[1]
    experts = lax.axis_size("expert")
    pipes = lax.axis_size("pipe")
    everyone = ("pipe", "expert")
    cap = tok_dev // (2 * experts)
    scale = 1.0 / math.sqrt(head)
    f32, bf16 = jnp.float32, jnp.bfloat16
    both_weights = jnp.concatenate([key_weight, value_weight], axis=1)
    own_kv = jnp.dot(enc_states, both_weights, preferred_element_type=f32).astype(bf16)
    blocks = [own_kv] + [shifted(own_kv, "pipe", s) for s in range(1, pipes)]
    kv = jnp.concatenate(blocks, axis=0)
    keys, values = kv[:, :head], kv[:, head:]
    owner = lax.rem(lax.axis_index("pipe") + pipes - jnp.arange(pipes, dtype=jnp.int32), pipes)
    position = (owner[:, None] * enc_dev + jnp.arange(enc_dev, dtype=jnp.int32)[None, :]).reshape(-1)
    scores = (
        lax.dot_general(keys, queries, (((1,), (1,)), ((), ())), preferred_element_type=f32) * scale
    )
    visible = position[:, None] < lengths[None, :]
    scores = jnp.where(visible, scores, -1e30)
    highest = jnp.max(scores, axis=0, keepdims=True)
    weights = jnp.where(visible, jnp.exp(scores - highest), 0.0)
    probs = weights / jnp.sum(weights, axis=0, keepdims=True)
    probs_low = probs.astype(bf16)
    context = lax.dot_general(
        values, probs_low, (((0,), (0,)), ((), ())), preferred_element_type=f32
    ).astype(bf16)
    context_blocks = context.reshape(head, experts, tok_dev).transpose(1, 0, 2)
    gathered = lax.all_to_all(context_blocks, "expert", split_axis=0, concat_axis=0, tiled=True)
    hidden_state = residual.astype(f32) + gathered.reshape(model, tok_dev).T.astype(f32)
    power = jnp.mean(hidden_state * hidden_state, axis=1, keepdims=True)
    normed = (hidden_state * lax.rsqrt(power + 1e-06) * norm_gain.astype(f32)).astype(bf16)
    expert_ids = routes[:, 0]
    onehot = (expert_ids[:, None] == jnp.arange(experts, dtype=jnp.int32)[None, :]).astype(
        jnp.int32
    )
    slot_rank = jnp.sum((jnp.cumsum(onehot, axis=0) - onehot) * onehot, axis=1)
    target = jnp.where(slot_rank < cap, expert_ids * cap + slot_rank, -1)
    placing = (jnp.arange(experts * cap, dtype=jnp.int32)[:, None] == target[None, :]).astype(bf16)
    outgoing = jnp.dot(placing, normed, preferred_element_type=f32).astype(bf16)
    outgoing = jnp.broadcast_to(
        outgoing.reshape(1, experts, cap, model), (pipes, experts, cap, model)
    ).reshape(pipes * experts, cap, model)
    arrived = lax.all_to_all(outgoing, everyone, split_axis=0, concat_axis=0, tiled=True)
    active = jnp.maximum(
        jnp.dot(
            arrived.reshape(pipes * experts * cap, model), w_in[0], preferred_element_type=f32
        ),
        0.0,
    ).astype(bf16)
    part = jnp.dot(active, w_out[0], preferred_element_type=f32).astype(bf16)
    returned = lax.all_to_all(
        part.reshape(pipes * experts, cap, model),
        everyone,
        split_axis=0,
        concat_axis=0,
        tiled=True,
    ).reshape(pipes, experts * cap, model)
    expert_rows = jnp.sum(returned.astype(f32), axis=0).astype(bf16)
    expert_out = lax.dot_general(
        placing, expert_rows, (((0,), (0,)), ((), ())), preferred_element_type=f32
    )
    layer_out = (hidden_state + expert_out).astype(bf16)

    grad_values = jnp.dot(probs_low, context_grad, preferred_element_type=f32)
    grad_probs = lax.dot_general(
        values, context_grad, (((1,), (1,)), ((), ())), preferred_element_type=f32
    )
    row_delta = jnp.sum(probs * grad_probs, axis=0, keepdims=True)
    grad_scores = (probs * (grad_probs - row_delta) * scale).astype(bf16)
    grad_keys = jnp.dot(grad_scores, queries, preferred_element_type=f32)
    grads = jnp.concatenate([grad_keys, grad_values], axis=1)
    total = grads[:enc_dev]
    for s in range(1, pipes):
        total = total + shifted(grads[s * enc_dev : (s + 1) * enc_dev], "pipe", -s)
    enc_part = lax.dot_general(
        total.astype(bf16), both_weights, (((1,), (1,)), ((), ())), preferred_element_type=f32
    )
    parts = lax.all_to_all(
        jnp.broadcast_to(enc_part[None], (experts, enc_dev, model)),
        "expert",
        split_axis=0,
        concat_axis=0,
        tiled=True,
    )
    enc_grad = jnp.sum(parts, axis=0).astype(bf16)
    return (layer_out, enc_grad)


def solution(mesh):
    placed = (
        P("pipe", None),
        P(None, "expert"),
        P(None, "expert"),
        P("pipe", "expert"),
        P("pipe"),
        P("pipe", "expert"),
        P(("pipe", "expert"), None),
        P(),
        P(("pipe", "expert"), None),
        P("expert", None, "pipe"),
        P("expert", "pipe", None),
    )
    return jax.shard_map(
        per_device,
        mesh=mesh,
        in_specs=placed,
        out_specs=(P(("pipe", "expert"), None), P("pipe", None)),
        check_vma=False,
    )
```

```python
import functools
import math

import jax
import jax.numpy as jnp
from jax import lax
from jax.experimental import pallas as pl
from jax.experimental.pallas import tpu as pltpu
from jax.sharding import PartitionSpec as P

EVERYONE = ("pipe", "expert")
VMEM = pl.BlockSpec(memory_space=pltpu.VMEM)
HBM = pl.BlockSpec(memory_space=pltpu.HBM)


def shifted(value, axis, step):
    size = lax.axis_size(axis)
    return lax.ppermute(value, axis, [(i, (i + step) % size) for i in range(size)])


def crossed(value, bit):
    size = lax.axis_size("expert")
    return lax.ppermute(value, "expert", [(i, i ^ bit) for i in range(size)])


def pick_half(ref, bit, mine):
    half = ref.shape[1] // 2
    side = lax.rem(lax.axis_index("expert") // bit, 2)
    return ref[:, pl.ds(pl.multiple_of((side if mine else 1 - side) * half, half), half)]


def project_kernel(
    cap, enc_hbm, key_hbm, value_hbm, queries_hbm, lengths_hbm, gain_hbm, routes_hbm, residual_hbm, *refs
):
    spread_hbm, keep_ref, send_ref, lengths_ref, gain_ref, target_ref, residual_ref = refs[:7]
    enc_ref, key_ref, value_ref, queries_ref, routes_ref, spread_ref, arrived, left = refs[7:]
    f32, bf16 = jnp.float32, jnp.bfloat16
    here, experts = lax.axis_index("expert"), lax.axis_size("expert")
    tok_dev = routes_ref.shape[1]
    own_tokens = pl.ds(pl.multiple_of(here * tok_dev, tok_dev), tok_dev)
    fetches = [
        pltpu.make_async_copy(source, target, arrived.at[i])
        for i, (source, target) in enumerate(
            (
                (enc_hbm, enc_ref),
                (key_hbm, key_ref),
                (value_hbm, value_ref),
                (routes_hbm, routes_ref),
                (queries_hbm, queries_ref),
                (lengths_hbm.at[own_tokens], lengths_ref),
                (gain_hbm, gain_ref),
                (residual_hbm, residual_ref),
            )
        )
    ]
    for fetch in fetches:
        fetch.start()
    for fetch in fetches[:3]:
        fetch.wait()
    enc = enc_ref[...]
    own = jnp.concatenate(
        [
            lax.dot_general(enc, ref[...], (((1,), (1,)), ((), ())), preferred_element_type=f32)
            for ref in (key_ref, value_ref)
        ],
        axis=1,
    )
    spread_ref[...] = jnp.broadcast_to(own.astype(bf16)[None], spread_ref.shape)
    leave = pltpu.make_async_copy(spread_ref, spread_hbm, left)
    leave.start()
    for fetch in fetches[3:]:
        fetch.wait()
    keep_ref[...] = pick_half(queries_ref, experts // 2, True)
    send_ref[...] = pick_half(queries_ref, experts // 2, False)
    routes = routes_ref[...]
    onehot = lax.broadcasted_iota(jnp.int32, (experts, tok_dev), 0) == routes
    earlier = lax.broadcasted_iota(jnp.int32, (tok_dev, tok_dev), 0) < lax.broadcasted_iota(
        jnp.int32, (tok_dev, tok_dev), 1
    )
    before = jnp.dot(
        onehot.astype(f32).astype(bf16), earlier.astype(f32).astype(bf16), preferred_element_type=f32
    )
    slot_rank = jnp.sum(jnp.where(onehot, before, 0.0), axis=0, keepdims=True).astype(jnp.int32)
    target_ref[...] = jnp.where(slot_rank < cap, routes * cap + slot_rank, -1)
    leave.wait()


def split_kernel(bit, kept_ref, got_ref, keep_ref, send_ref):
    rows = kept_ref.shape[0]
    for first, ref in ((0, kept_ref), (rows, got_ref)):
        keep_ref[first : first + rows] = pick_half(ref, bit, True)
        send_ref[first : first + rows] = pick_half(ref, bit, False)


def block_kernel(group, kv_ref, keys_ref, values_ref):
    pipes, heads, enc_dev, wide = kv_ref.shape
    head = wide // 2
    rows, cols = pipes * group * enc_dev, group * head
    f32, bf16 = jnp.float32, jnp.bfloat16
    row_head = lax.rem(lax.broadcasted_iota(jnp.int32, (rows, cols), 0) // enc_dev, group)
    same_head = row_head == lax.broadcasted_iota(jnp.int32, (rows, cols), 1) // head
    left = lax.broadcasted_iota(jnp.int32, (rows, wide), 1) < head
    for part in range(heads // group):
        kv = kv_ref[:, part * group : (part + 1) * group].reshape(rows, wide).astype(f32)
        turned = pltpu.roll(kv, head, 1)
        twice_keys = jnp.where(left, kv, turned).astype(bf16)
        twice_values = jnp.where(left, turned, kv).astype(bf16)
        for twice, ref in ((twice_keys, keys_ref), (twice_values, values_ref)):
            block = jnp.concatenate([twice] * (group // 2), axis=1)
            ref[part] = jnp.where(same_head, block, jnp.zeros_like(block))


def attend_kernel(
    scale,
    enc_dev,
    head,
    keys_ref,
    values_ref,
    lengths_ref,
    residual_ref,
    gain_ref,
    target_ref,
    kept_ref,
    got_ref,
    hidden_ref,
    out_ref,
    q_ref,
):
    parts, rows, cols = keys_ref.shape
    group, heads = cols // head, parts * cols // head
    pipes, tok_dev = rows // (group * enc_dev), q_ref.shape[1]
    f32, bf16 = jnp.float32, jnp.bfloat16
    here = lax.axis_index("expert")
    levels = heads.bit_length() - 1
    for r in range(heads):
        flips = sum(1 << (levels - 1 - i) for i in range(levels) if r >> i & 1)
        which = pl.multiple_of(lax.bitwise_xor(here, flips) * head, head)
        ref, first = (kept_ref, r) if r < heads // 2 else (got_ref, r - heads // 2)
        q_ref[pl.ds(which, head)] = ref[first * head : (first + 1) * head]
    shape = (pipes, group, enc_dev, tok_dev)
    position = lax.broadcasted_iota(jnp.int32, shape, 0) * enc_dev + lax.broadcasted_iota(
        jnp.int32, shape, 2
    )
    visible = position < lengths_ref[...].reshape(1, 1, 1, tok_dev)
    pieces = []
    for part in range(parts):
        scores = scale * jnp.dot(
            keys_ref[part], q_ref[part * cols : (part + 1) * cols], preferred_element_type=f32
        )
        scores = jnp.where(visible, scores.reshape(shape), -1e30)
        highest = jnp.max(jnp.max(scores, axis=0, keepdims=True), axis=2, keepdims=True)
        weights = jnp.where(visible, jnp.exp(scores - highest), 0.0)
        total = jnp.sum(jnp.sum(weights, axis=0, keepdims=True), axis=2, keepdims=True)
        probs_low = (weights / total).reshape(rows, tok_dev).astype(bf16)
        pieces.append(
            lax.dot_general(
                probs_low, values_ref[part], (((0,), (0,)), ((), ())), preferred_element_type=f32
            ).astype(bf16)
        )
    context = pieces[0] if len(pieces) == 1 else jnp.concatenate(pieces, axis=1)
    hidden = residual_ref[...].astype(f32) + context.astype(f32)
    hidden_ref[...] = hidden
    power = jnp.mean(hidden * hidden, axis=1, keepdims=True)
    normed = (hidden * lax.rsqrt(power + 1e-06) * gain_ref[...].astype(f32).reshape(1, -1)).astype(
        bf16
    )
    slots = out_ref.shape[1]
    placing = lax.broadcasted_iota(jnp.int32, (slots, tok_dev), 0) == target_ref[...]
    outgoing = jnp.dot(
        placing.astype(f32).astype(bf16), normed, preferred_element_type=f32
    ).astype(bf16)
    for pipe in range(pipes):
        out_ref[pipe] = outgoing


def backward_kernel(scale, kv_ref, queries_ref, grad_ref, lengths_ref, *refs):
    out_refs, sums_ref = refs[:-1], refs[-1]
    pipes, _, enc_dev, wide = kv_ref.shape
    head, rows = wide // 2, pipes * enc_dev
    f32, bf16 = jnp.float32, jnp.bfloat16
    kv = kv_ref[:, lax.axis_index("expert")].reshape(rows, wide)
    queries, grads = queries_ref[...], grad_ref[...]
    tokens = queries.shape[1]
    keys, values = kv[:, :head], kv[:, head:]
    scores = jnp.dot(keys, queries, preferred_element_type=f32) * scale
    visible = lax.broadcasted_iota(jnp.int32, (rows, tokens), 0) < lengths_ref[...].reshape(1, tokens)
    scores = jnp.where(visible, scores, -1e30)
    highest = jnp.max(scores, axis=0, keepdims=True)
    weights = jnp.where(visible, jnp.exp(scores - highest), 0.0)
    probs = weights / jnp.sum(weights, axis=0, keepdims=True)
    probs_low = probs.astype(bf16)
    grad_probs = jnp.dot(values, grads, preferred_element_type=f32)
    row_delta = jnp.sum(probs * grad_probs, axis=0, keepdims=True)
    grad_scores = (probs * (grad_probs - row_delta) * scale).astype(bf16)
    over_tokens = (((1,), (1,)), ((), ()))
    grad_keys = lax.dot_general(grad_scores, queries, over_tokens, preferred_element_type=f32)
    grad_values = lax.dot_general(probs_low, grads, over_tokens, preferred_element_type=f32)
    sums_ref[...] = jnp.concatenate([grad_keys, grad_values], axis=1).reshape(sums_ref.shape)
    own = lax.axis_index("pipe")
    for s, out_ref in enumerate(out_refs):
        out_ref[...] = sums_ref[lax.rem(own + s, pipes)]


def combine_kernel(returned_ref, target_ref, hidden_ref, out_ref):
    slots, tok_dev = returned_ref.shape[1], hidden_ref.shape[0]
    f32, bf16 = jnp.float32, jnp.bfloat16
    rows = jnp.sum(returned_ref[...].astype(f32), axis=0).astype(bf16)
    placing = lax.broadcasted_iota(jnp.int32, (slots, tok_dev), 0) == target_ref[...]
    expert_out = lax.dot_general(
        placing.astype(f32).astype(bf16), rows, (((0,), (0,)), ((), ())), preferred_element_type=f32
    )
    out_ref[...] = (hidden_ref[...] + expert_out).astype(bf16)


def per_device(
    enc_states,
    key_weight,
    value_weight,
    queries,
    lengths,
    context_grad,
    residual,
    norm_gain,
    routes,
    w_in,
    w_out,
):
    enc_dev = enc_states.shape[0]
    head = key_weight.shape[1]
    tok_dev = residual.shape[0]
    model = residual.shape[1]
    experts = lax.axis_size("expert")
    pipes = lax.axis_size("pipe")
    cap = tok_dev // (2 * experts)
    scale = 1.0 / math.sqrt(head)
    f32, bf16 = jnp.float32, jnp.bfloat16
    here, own_pipe = lax.axis_index("expert"), lax.axis_index("pipe")
    params = pltpu.CompilerParams(vmem_limit_bytes=(8 << 20) if model <= 1024 else (40 << 20))
    queries_turned = queries.T
    half = (head, experts * tok_dev // 2)
    spread_kv, keep, send, own_lengths, gain, target, near_residual = pl.pallas_call(
        functools.partial(project_kernel, cap),
        out_shape=[
            jax.ShapeDtypeStruct((pipes * experts, enc_dev, 2 * head), bf16),
            jax.ShapeDtypeStruct(half, bf16),
            jax.ShapeDtypeStruct(half, bf16),
            jax.ShapeDtypeStruct((tok_dev,), jnp.int32),
            jax.ShapeDtypeStruct((model,), bf16),
            jax.ShapeDtypeStruct((1, tok_dev), jnp.int32),
            jax.ShapeDtypeStruct((tok_dev, model), bf16),
        ],
        in_specs=[HBM] * 8,
        out_specs=[HBM] + [VMEM] * 6,
        scratch_shapes=[
            pltpu.VMEM((enc_dev, model), bf16),
            pltpu.VMEM((head, model), bf16),
            pltpu.VMEM((head, model), bf16),
            pltpu.VMEM((head, experts * tok_dev), bf16),
            pltpu.VMEM((1, tok_dev), jnp.int32),
            pltpu.VMEM((pipes * experts, enc_dev, 2 * head), bf16),
            pltpu.SemaphoreType.DMA((8,)),
            pltpu.SemaphoreType.DMA,
        ],
        compiler_params=params,
    )(
        *(
            pltpu.with_memory_space_constraint(value, pltpu.HBM)
            for value in (
                enc_states,
                key_weight.T,
                value_weight.T,
                queries_turned,
                lengths,
                norm_gain,
                routes.T,
                residual,
            )
        )
    )
    kv = lax.all_to_all(
        spread_kv, EVERYONE, split_axis=0, concat_axis=0, tiled=True
    ).reshape(pipes, experts, enc_dev, 2 * head)
    bit = experts // 2
    got = crossed(send, bit)
    while bit > 1:
        bit //= 2
        keep, send = pl.pallas_call(
            functools.partial(split_kernel, bit),
            out_shape=[jax.ShapeDtypeStruct((2 * keep.shape[0], keep.shape[1] // 2), bf16)] * 2,
            in_specs=[VMEM] * 2,
            out_specs=[VMEM] * 2,
            compiler_params=params,
            cost_estimate=pl.CostEstimate(flops=0, bytes_accessed=0, transcendentals=0),
        )(keep, got)
        got = crossed(send, bit)
    group = max(g for g in range(2, experts + 1, 2) if experts % g == 0 and g * head <= 512)
    blocks = (experts // group, pipes * group * enc_dev, group * head)
    key_blocks, value_blocks = pl.pallas_call(
        functools.partial(block_kernel, group),
        out_shape=[jax.ShapeDtypeStruct(blocks, bf16)] * 2,
        in_specs=[VMEM],
        out_specs=[VMEM] * 2,
        compiler_params=params,
        cost_estimate=pl.CostEstimate(flops=1 << 34, bytes_accessed=1 << 26, transcendentals=0),
    )(kv)
    hidden_state, outgoing = pl.pallas_call(
        functools.partial(attend_kernel, scale, enc_dev, head),
        out_shape=(
            jax.ShapeDtypeStruct((tok_dev, model), f32),
            jax.ShapeDtypeStruct((pipes, experts * cap, model), bf16),
        ),
        in_specs=[VMEM] * 8,
        out_specs=[VMEM] * 2,
        scratch_shapes=[pltpu.VMEM((model, tok_dev), bf16)],
        compiler_params=params,
    )(key_blocks, value_blocks, own_lengths, near_residual, gain, target, keep, got)
    outgoing = outgoing.reshape(pipes * experts, cap, model)
    kv, outgoing = lax.optimization_barrier((kv, outgoing))
    total, *others = pl.pallas_call(
        functools.partial(backward_kernel, scale),
        out_shape=[jax.ShapeDtypeStruct((enc_dev, 2 * head), f32)] * pipes,
        in_specs=[VMEM] * 4,
        out_specs=[VMEM] * pipes,
        scratch_shapes=[pltpu.VMEM((pipes, enc_dev, 2 * head), f32)],
        compiler_params=params,
        cost_estimate=pl.CostEstimate(flops=0, bytes_accessed=0, transcendentals=0),
    )(kv, queries_turned, context_grad.T, lengths)
    for s, other in enumerate(others):
        total = total + shifted(other, "pipe", s + 1)
    total = total.astype(bf16)
    arrived = lax.all_to_all(outgoing, EVERYONE, split_axis=0, concat_axis=0, tiled=True)
    active = jnp.maximum(
        jnp.dot(
            arrived.reshape(pipes * experts * cap, model), w_in[0], preferred_element_type=f32
        ),
        0.0,
    ).astype(bf16)
    part = jnp.dot(active, w_out[0], preferred_element_type=f32).astype(bf16)
    enc_part = lax.dot_general(
        total[:, :head], key_weight, (((1,), (1,)), ((), ())), preferred_element_type=f32
    ) + lax.dot_general(
        total[:, head:], value_weight, (((1,), (1,)), ((), ())), preferred_element_type=f32
    )
    returned = lax.all_to_all(
        part.reshape(pipes * experts, cap, model),
        EVERYONE,
        split_axis=0,
        concat_axis=0,
        tiled=True,
    ).reshape(pipes, experts * cap, model)
    layer_out = pl.pallas_call(
        combine_kernel,
        out_shape=jax.ShapeDtypeStruct((tok_dev, model), bf16),
        in_specs=[VMEM] * 3,
        out_specs=VMEM,
        compiler_params=params,
    )(returned, target, hidden_state)
    for level in range(experts.bit_length() - 1):
        enc_part = enc_part + crossed(enc_part, 1 << level)
    enc_grad = enc_part.astype(bf16)
    return (layer_out, enc_grad)


def solution(mesh):
    placed = (
        P("pipe", None),
        P(None, "expert"),
        P(None, "expert"),
        P("pipe", "expert"),
        P("pipe"),
        P("pipe", "expert"),
        P(("pipe", "expert"), None),
        P(),
        P(("pipe", "expert"), None),
        P("expert", None, "pipe"),
        P("expert", "pipe", None),
    )
    return jax.shard_map(
        per_device,
        mesh=mesh,
        in_specs=placed,
        out_specs=(P(("pipe", "expert"), None), P("pipe", None)),
        check_vma=False,
    )
```

```python
import functools
import math

import jax
import jax.numpy as jnp
from jax import lax
from jax.experimental import pallas as pl
from jax.experimental.pallas import tpu as pltpu
from jax.sharding import PartitionSpec as P

EVERYONE = ("pipe", "expert")
VMEM = pl.BlockSpec(memory_space=pltpu.VMEM)
HBM = pl.BlockSpec(memory_space=pltpu.HBM)


def shifted(value, axis, step):
    size = lax.axis_size(axis)
    return lax.ppermute(value, axis, [(i, (i + step) % size) for i in range(size)])


def crossed(value, bit):
    size = lax.axis_size("expert")
    return lax.ppermute(value, "expert", [(i, i ^ bit) for i in range(size)])


def project_kernel(
    cap, enc_hbm, key_hbm, value_hbm, queries_hbm, lengths_hbm, gain_hbm, routes_hbm, residual_hbm, *refs
):
    spread_hbm, keep_ref, send_ref, lengths_ref, gain_ref, target_ref, residual_ref = refs[:7]
    enc_ref, key_ref, value_ref, queries_ref, routes_ref, spread_ref, arrived, left = refs[7:]
    f32, bf16 = jnp.float32, jnp.bfloat16
    here, experts = lax.axis_index("expert"), lax.axis_size("expert")
    tok_dev = routes_ref.shape[1]
    own_tokens = pl.ds(pl.multiple_of(here * tok_dev, tok_dev), tok_dev)
    fetches = [
        pltpu.make_async_copy(source, target, arrived.at[i])
        for i, (source, target) in enumerate(
            (
                (enc_hbm, enc_ref),
                (key_hbm, key_ref),
                (value_hbm, value_ref),
                (routes_hbm, routes_ref),
                (queries_hbm, queries_ref),
                (lengths_hbm.at[own_tokens], lengths_ref),
                (gain_hbm, gain_ref),
                (residual_hbm, residual_ref),
            )
        )
    ]
    for fetch in fetches:
        fetch.start()
    for fetch in fetches[:3]:
        fetch.wait()
    enc = enc_ref[...]
    own = jnp.concatenate(
        [
            lax.dot_general(enc, ref[...], (((1,), (1,)), ((), ())), preferred_element_type=f32)
            for ref in (key_ref, value_ref)
        ],
        axis=1,
    )
    spread_ref[...] = jnp.broadcast_to(own.astype(bf16)[None], spread_ref.shape)
    leave = pltpu.make_async_copy(spread_ref, spread_hbm, left)
    leave.start()
    for fetch in fetches[3:]:
        fetch.wait()
    core = lax.rem(here, 2)
    for chip in range(experts // 2):
        for ref, which in ((keep_ref, core), (send_ref, 1 - core)):
            lanes = pl.ds(pl.multiple_of((2 * chip + which) * tok_dev, tok_dev), tok_dev)
            ref[chip] = queries_ref[:, lanes]
    routes = routes_ref[...]
    onehot = lax.broadcasted_iota(jnp.int32, (experts, tok_dev), 0) == routes
    earlier = lax.broadcasted_iota(jnp.int32, (tok_dev, tok_dev), 0) < lax.broadcasted_iota(
        jnp.int32, (tok_dev, tok_dev), 1
    )
    before = jnp.dot(
        onehot.astype(f32).astype(bf16), earlier.astype(f32).astype(bf16), preferred_element_type=f32
    )
    slot_rank = jnp.sum(jnp.where(onehot, before, 0.0), axis=0, keepdims=True).astype(jnp.int32)
    target_ref[...] = jnp.where(slot_rank < cap, routes * cap + slot_rank, -1)
    leave.wait()


def gather_kernel(keep_ref, got_ref, *out_refs):
    chip = lax.axis_index("expert") // 2
    head = keep_ref.shape[1]
    for k, out_ref in enumerate(out_refs):
        out_ref[:head] = keep_ref[lax.bitwise_xor(chip, k)]
        out_ref[head:] = got_ref[lax.bitwise_xor(chip, k)]


def block_kernel(group, kv_ref, keys_ref, values_ref):
    pipes, heads, enc_dev, wide = kv_ref.shape
    head = wide // 2
    rows, cols = pipes * group * enc_dev, group * head
    f32, bf16 = jnp.float32, jnp.bfloat16
    row_head = lax.rem(lax.broadcasted_iota(jnp.int32, (rows, cols), 0) // enc_dev, group)
    same_head = row_head == lax.broadcasted_iota(jnp.int32, (rows, cols), 1) // head
    left = lax.broadcasted_iota(jnp.int32, (rows, wide), 1) < head
    for part in range(heads // group):
        kv = kv_ref[:, part * group : (part + 1) * group].reshape(rows, wide).astype(f32)
        turned = pltpu.roll(kv, head, 1)
        twice_keys = jnp.where(left, kv, turned).astype(bf16)
        twice_values = jnp.where(left, turned, kv).astype(bf16)
        for twice, ref in ((twice_keys, keys_ref), (twice_values, values_ref)):
            block = jnp.concatenate([twice] * (group // 2), axis=1)
            ref[part] = jnp.where(same_head, block, jnp.zeros_like(block))


def attend_kernel(
    scale, enc_dev, head, keys_ref, values_ref, lengths_ref, residual_ref, gain_ref, target_ref, *refs
):
    parts, rows, cols = keys_ref.shape
    group, heads = cols // head, parts * cols // head
    *query_refs, hidden_ref, out_ref, q_ref = refs
    pipes, tok_dev = rows // (group * enc_dev), q_ref.shape[1]
    f32, bf16 = jnp.float32, jnp.bfloat16
    here = lax.axis_index("expert")
    for k, ref in zip((0, *range(len(query_refs) - 1, 0, -1)), query_refs, strict=True):
        for i in range(2):
            which = pl.multiple_of(lax.bitwise_xor(here, 2 * k + i) * head, head)
            q_ref[pl.ds(which, head)] = ref[i * head : (i + 1) * head]
    shape = (pipes, group, enc_dev, tok_dev)
    position = lax.broadcasted_iota(jnp.int32, shape, 0) * enc_dev + lax.broadcasted_iota(
        jnp.int32, shape, 2
    )
    visible = position < lengths_ref[...].reshape(1, 1, 1, tok_dev)
    pieces = []
    for part in range(parts):
        scores = scale * jnp.dot(
            keys_ref[part], q_ref[part * cols : (part + 1) * cols], preferred_element_type=f32
        )
        scores = jnp.where(visible, scores.reshape(shape), -1e30)
        highest = jnp.max(jnp.max(scores, axis=0, keepdims=True), axis=2, keepdims=True)
        weights = jnp.where(visible, jnp.exp(scores - highest), 0.0)
        total = jnp.sum(jnp.sum(weights, axis=0, keepdims=True), axis=2, keepdims=True)
        probs_low = (weights / total).reshape(rows, tok_dev).astype(bf16)
        pieces.append(
            lax.dot_general(
                probs_low, values_ref[part], (((0,), (0,)), ((), ())), preferred_element_type=f32
            ).astype(bf16)
        )
    context = pieces[0] if len(pieces) == 1 else jnp.concatenate(pieces, axis=1)
    hidden = residual_ref[...].astype(f32) + context.astype(f32)
    hidden_ref[...] = hidden
    power = jnp.mean(hidden * hidden, axis=1, keepdims=True)
    normed = (hidden * lax.rsqrt(power + 1e-06) * gain_ref[...].astype(f32).reshape(1, -1)).astype(
        bf16
    )
    slots = out_ref.shape[1]
    placing = lax.broadcasted_iota(jnp.int32, (slots, tok_dev), 0) == target_ref[...]
    outgoing = jnp.dot(
        placing.astype(f32).astype(bf16), normed, preferred_element_type=f32
    ).astype(bf16)
    for pipe in range(pipes):
        out_ref[pipe] = outgoing


def backward_kernel(scale, kv_ref, queries_ref, grad_ref, lengths_ref, *refs):
    out_refs, sums_ref = refs[:-1], refs[-1]
    pipes, _, enc_dev, wide = kv_ref.shape
    head, rows = wide // 2, pipes * enc_dev
    f32, bf16 = jnp.float32, jnp.bfloat16
    kv = kv_ref[:, lax.axis_index("expert")].reshape(rows, wide)
    queries, grads = queries_ref[...], grad_ref[...]
    tokens = queries.shape[1]
    keys, values = kv[:, :head], kv[:, head:]
    scores = jnp.dot(keys, queries, preferred_element_type=f32) * scale
    visible = lax.broadcasted_iota(jnp.int32, (rows, tokens), 0) < lengths_ref[...].reshape(1, tokens)
    scores = jnp.where(visible, scores, -1e30)
    highest = jnp.max(scores, axis=0, keepdims=True)
    weights = jnp.where(visible, jnp.exp(scores - highest), 0.0)
    probs = weights / jnp.sum(weights, axis=0, keepdims=True)
    probs_low = probs.astype(bf16)
    grad_probs = jnp.dot(values, grads, preferred_element_type=f32)
    row_delta = jnp.sum(probs * grad_probs, axis=0, keepdims=True)
    grad_scores = (probs * (grad_probs - row_delta) * scale).astype(bf16)
    over_tokens = (((1,), (1,)), ((), ()))
    grad_keys = lax.dot_general(grad_scores, queries, over_tokens, preferred_element_type=f32)
    grad_values = lax.dot_general(probs_low, grads, over_tokens, preferred_element_type=f32)
    sums_ref[...] = jnp.concatenate([grad_keys, grad_values], axis=1).reshape(sums_ref.shape)
    own = lax.axis_index("pipe")
    for s, out_ref in enumerate(out_refs):
        out_ref[...] = sums_ref[lax.rem(own + s, pipes)]


def combine_kernel(returned_ref, target_ref, hidden_ref, out_ref):
    slots, tok_dev = returned_ref.shape[1], hidden_ref.shape[0]
    f32, bf16 = jnp.float32, jnp.bfloat16
    rows = jnp.sum(returned_ref[...].astype(f32), axis=0).astype(bf16)
    placing = lax.broadcasted_iota(jnp.int32, (slots, tok_dev), 0) == target_ref[...]
    expert_out = lax.dot_general(
        placing.astype(f32).astype(bf16), rows, (((0,), (0,)), ((), ())), preferred_element_type=f32
    )
    out_ref[...] = (hidden_ref[...] + expert_out).astype(bf16)


def per_device(
    enc_states,
    key_weight,
    value_weight,
    queries,
    lengths,
    context_grad,
    residual,
    norm_gain,
    routes,
    w_in,
    w_out,
):
    enc_dev = enc_states.shape[0]
    head = key_weight.shape[1]
    tok_dev = residual.shape[0]
    model = residual.shape[1]
    experts = lax.axis_size("expert")
    pipes = lax.axis_size("pipe")
    cap = tok_dev // (2 * experts)
    scale = 1.0 / math.sqrt(head)
    f32, bf16 = jnp.float32, jnp.bfloat16
    here, own_pipe = lax.axis_index("expert"), lax.axis_index("pipe")
    params = pltpu.CompilerParams(vmem_limit_bytes=(8 << 20) if model <= 1024 else (40 << 20))
    queries_turned = queries.T
    half = (experts // 2, head, tok_dev)
    spread_kv, keep, send, own_lengths, gain, target, near_residual = pl.pallas_call(
        functools.partial(project_kernel, cap),
        out_shape=[
            jax.ShapeDtypeStruct((pipes * experts, enc_dev, 2 * head), bf16),
            jax.ShapeDtypeStruct(half, bf16),
            jax.ShapeDtypeStruct(half, bf16),
            jax.ShapeDtypeStruct((tok_dev,), jnp.int32),
            jax.ShapeDtypeStruct((model,), bf16),
            jax.ShapeDtypeStruct((1, tok_dev), jnp.int32),
            jax.ShapeDtypeStruct((tok_dev, model), bf16),
        ],
        in_specs=[HBM] * 8,
        out_specs=[HBM] + [VMEM] * 6,
        scratch_shapes=[
            pltpu.VMEM((enc_dev, model), bf16),
            pltpu.VMEM((head, model), bf16),
            pltpu.VMEM((head, model), bf16),
            pltpu.VMEM((head, experts * tok_dev), bf16),
            pltpu.VMEM((1, tok_dev), jnp.int32),
            pltpu.VMEM((pipes * experts, enc_dev, 2 * head), bf16),
            pltpu.SemaphoreType.DMA((8,)),
            pltpu.SemaphoreType.DMA,
        ],
        compiler_params=params,
    )(
        *(
            pltpu.with_memory_space_constraint(value, pltpu.HBM)
            for value in (
                enc_states,
                key_weight.T,
                value_weight.T,
                queries_turned,
                lengths,
                norm_gain,
                routes.T,
                residual,
            )
        )
    )
    kv = lax.all_to_all(
        spread_kv, EVERYONE, split_axis=0, concat_axis=0, tiled=True
    ).reshape(pipes, experts, enc_dev, 2 * head)
    chips = experts // 2
    query_blocks = pl.pallas_call(
        gather_kernel,
        out_shape=[jax.ShapeDtypeStruct((2 * head, tok_dev), bf16)] * chips,
        in_specs=[VMEM] * 2,
        out_specs=[VMEM] * chips,
        compiler_params=params,
        cost_estimate=pl.CostEstimate(flops=1 << 34, bytes_accessed=1 << 26, transcendentals=0),
    )(keep, crossed(send, 1))
    query_blocks = [query_blocks[0]] + [crossed(query_blocks[k], 2 * k) for k in range(1, chips)]
    group = max(g for g in range(2, experts + 1, 2) if experts % g == 0 and g * head <= 512)
    blocks = (experts // group, pipes * group * enc_dev, group * head)
    key_blocks, value_blocks = pl.pallas_call(
        functools.partial(block_kernel, group),
        out_shape=[jax.ShapeDtypeStruct(blocks, bf16)] * 2,
        in_specs=[VMEM],
        out_specs=[VMEM] * 2,
        compiler_params=params,
        cost_estimate=pl.CostEstimate(flops=1 << 34, bytes_accessed=1 << 26, transcendentals=0),
    )(kv)
    hidden_state, outgoing = pl.pallas_call(
        functools.partial(attend_kernel, scale, enc_dev, head),
        out_shape=(
            jax.ShapeDtypeStruct((tok_dev, model), f32),
            jax.ShapeDtypeStruct((pipes, experts * cap, model), bf16),
        ),
        in_specs=[VMEM] * (6 + chips),
        out_specs=[VMEM] * 2,
        scratch_shapes=[pltpu.VMEM((model, tok_dev), bf16)],
        compiler_params=params,
    )(key_blocks, value_blocks, own_lengths, near_residual, gain, target, query_blocks[0], *query_blocks[:0:-1])
    outgoing = outgoing.reshape(pipes * experts, cap, model)
    kv, outgoing = lax.optimization_barrier((kv, outgoing))
    total, *others = pl.pallas_call(
        functools.partial(backward_kernel, scale),
        out_shape=[jax.ShapeDtypeStruct((enc_dev, 2 * head), f32)] * pipes,
        in_specs=[VMEM] * 4,
        out_specs=[VMEM] * pipes,
        scratch_shapes=[pltpu.VMEM((pipes, enc_dev, 2 * head), f32)],
        compiler_params=params,
        cost_estimate=pl.CostEstimate(flops=0, bytes_accessed=0, transcendentals=0),
    )(kv, queries_turned, context_grad.T, lengths)
    for s, other in enumerate(others):
        total = total + shifted(other, "pipe", s + 1)
    total = total.astype(bf16)
    arrived = lax.all_to_all(outgoing, EVERYONE, split_axis=0, concat_axis=0, tiled=True)
    active = jnp.maximum(
        jnp.dot(
            arrived.reshape(pipes * experts * cap, model), w_in[0], preferred_element_type=f32
        ),
        0.0,
    ).astype(bf16)
    part = jnp.dot(active, w_out[0], preferred_element_type=f32).astype(bf16)
    enc_part = lax.dot_general(
        total[:, :head], key_weight, (((1,), (1,)), ((), ())), preferred_element_type=f32
    ) + lax.dot_general(
        total[:, head:], value_weight, (((1,), (1,)), ((), ())), preferred_element_type=f32
    )
    returned = lax.all_to_all(
        part.reshape(pipes * experts, cap, model),
        EVERYONE,
        split_axis=0,
        concat_axis=0,
        tiled=True,
    ).reshape(pipes, experts * cap, model)
    layer_out = pl.pallas_call(
        combine_kernel,
        out_shape=jax.ShapeDtypeStruct((tok_dev, model), bf16),
        in_specs=[VMEM] * 3,
        out_specs=VMEM,
        compiler_params=params,
    )(returned, target, hidden_state)
    for level in range(experts.bit_length() - 1):
        enc_part = enc_part + crossed(enc_part, 1 << level)
    enc_grad = enc_part.astype(bf16)
    return (layer_out, enc_grad)


def solution(mesh):
    placed = (
        P("pipe", None),
        P(None, "expert"),
        P(None, "expert"),
        P("pipe", "expert"),
        P("pipe"),
        P("pipe", "expert"),
        P(("pipe", "expert"), None),
        P(),
        P(("pipe", "expert"), None),
        P("expert", None, "pipe"),
        P("expert", "pipe", None),
    )
    return jax.shard_map(
        per_device,
        mesh=mesh,
        in_specs=placed,
        out_specs=(P(("pipe", "expert"), None), P("pipe", None)),
        check_vma=False,
    )
```

```python
import functools
import math

import jax
import jax.numpy as jnp
from jax import lax
from jax.experimental import pallas as pl
from jax.experimental.pallas import tpu as pltpu
from jax.sharding import PartitionSpec as P

EVERYONE = ("pipe", "expert")
VMEM = pl.BlockSpec(memory_space=pltpu.VMEM)
HBM = pl.BlockSpec(memory_space=pltpu.HBM)


def shifted(value, axis, step):
    size = lax.axis_size(axis)
    return lax.ppermute(value, axis, [(i, (i + step) % size) for i in range(size)])


def crossed(value, bit):
    size = lax.axis_size("expert")
    return lax.ppermute(value, "expert", [(i, i ^ bit) for i in range(size)])


def project_kernel(
    cap, enc_hbm, key_hbm, value_hbm, queries_hbm, lengths_hbm, gain_hbm, routes_hbm, residual_hbm, *refs
):
    spread_hbm, keep_ref, send_ref, lengths_ref, gain_ref, target_ref, residual_ref = refs[:7]
    enc_ref, key_ref, value_ref, queries_ref, routes_ref, spread_ref, arrived, left = refs[7:]
    f32, bf16 = jnp.float32, jnp.bfloat16
    here, experts = lax.axis_index("expert"), lax.axis_size("expert")
    tok_dev = routes_ref.shape[1]
    own_tokens = pl.ds(pl.multiple_of(here * tok_dev, tok_dev), tok_dev)
    fetches = [
        pltpu.make_async_copy(source, target, arrived.at[i])
        for i, (source, target) in enumerate(
            (
                (enc_hbm, enc_ref),
                (key_hbm, key_ref),
                (value_hbm, value_ref),
                (routes_hbm, routes_ref),
                (queries_hbm, queries_ref),
                (lengths_hbm.at[own_tokens], lengths_ref),
                (gain_hbm, gain_ref),
                (residual_hbm, residual_ref),
            )
        )
    ]
    for fetch in fetches:
        fetch.start()
    for fetch in fetches[:3]:
        fetch.wait()
    enc = enc_ref[...]
    own = jnp.concatenate(
        [
            lax.dot_general(enc, ref[...], (((1,), (1,)), ((), ())), preferred_element_type=f32)
            for ref in (key_ref, value_ref)
        ],
        axis=1,
    )
    spread_ref[...] = jnp.broadcast_to(own.astype(bf16)[None], spread_ref.shape)
    leave = pltpu.make_async_copy(spread_ref, spread_hbm, left)
    leave.start()
    for fetch in fetches[3:]:
        fetch.wait()
    core = lax.rem(here, 2)
    for chip in range(experts // 2):
        for ref, which in ((keep_ref, core), (send_ref, 1 - core)):
            lanes = pl.ds(pl.multiple_of((2 * chip + which) * tok_dev, tok_dev), tok_dev)
            ref[chip] = queries_ref[:, lanes]
    routes = routes_ref[...]
    onehot = lax.broadcasted_iota(jnp.int32, (experts, tok_dev), 0) == routes
    earlier = lax.broadcasted_iota(jnp.int32, (tok_dev, tok_dev), 0) < lax.broadcasted_iota(
        jnp.int32, (tok_dev, tok_dev), 1
    )
    before = jnp.dot(
        onehot.astype(f32).astype(bf16), earlier.astype(f32).astype(bf16), preferred_element_type=f32
    )
    slot_rank = jnp.sum(jnp.where(onehot, before, 0.0), axis=0, keepdims=True).astype(jnp.int32)
    target_ref[...] = jnp.where(slot_rank < cap, routes * cap + slot_rank, -1)
    leave.wait()


def gather_kernel(keep_ref, got_ref, *out_refs):
    chip = lax.axis_index("expert") // 2
    head = keep_ref.shape[1]
    for k, out_ref in enumerate(out_refs):
        out_ref[:head] = keep_ref[lax.bitwise_xor(chip, k)]
        out_ref[head:] = got_ref[lax.bitwise_xor(chip, k)]


def block_kernel(group, kv_ref, keys_ref, values_ref):
    pipes, heads, enc_dev, wide = kv_ref.shape
    head = wide // 2
    rows, cols = pipes * group * enc_dev, group * head
    f32, bf16 = jnp.float32, jnp.bfloat16
    row_head = lax.rem(lax.broadcasted_iota(jnp.int32, (rows, cols), 0) // enc_dev, group)
    same_head = row_head == lax.broadcasted_iota(jnp.int32, (rows, cols), 1) // head
    left = lax.broadcasted_iota(jnp.int32, (rows, wide), 1) < head
    for part in range(heads // group):
        kv = kv_ref[:, part * group : (part + 1) * group].reshape(rows, wide).astype(f32)
        turned = pltpu.roll(kv, head, 1)
        twice_keys = jnp.where(left, kv, turned).astype(bf16)
        twice_values = jnp.where(left, turned, kv).astype(bf16)
        for twice, ref in ((twice_keys, keys_ref), (twice_values, values_ref)):
            block = jnp.concatenate([twice] * (group // 2), axis=1)
            ref[part] = jnp.where(same_head, block, jnp.zeros_like(block))


def attend_kernel(
    scale, enc_dev, head, keys_ref, values_ref, lengths_ref, residual_ref, gain_ref, target_ref, *refs
):
    parts, rows, cols = keys_ref.shape
    group, heads = cols // head, parts * cols // head
    *query_refs, hidden_ref, out_ref, q_ref = refs
    pipes, tok_dev = rows // (group * enc_dev), q_ref.shape[1]
    f32, bf16 = jnp.float32, jnp.bfloat16
    here = lax.axis_index("expert")
    for k, ref in zip((0, *range(len(query_refs) - 1, 0, -1)), query_refs, strict=True):
        for i in range(2):
            which = pl.multiple_of(lax.bitwise_xor(here, 2 * k + i) * head, head)
            q_ref[pl.ds(which, head)] = ref[i * head : (i + 1) * head]
    shape = (pipes, group, enc_dev, tok_dev)
    position = lax.broadcasted_iota(jnp.int32, shape, 0) * enc_dev + lax.broadcasted_iota(
        jnp.int32, shape, 2
    )
    visible = position < lengths_ref[...].reshape(1, 1, 1, tok_dev)
    pieces = []
    for part in range(parts):
        scores = scale * jnp.dot(
            keys_ref[part], q_ref[part * cols : (part + 1) * cols], preferred_element_type=f32
        )
        scores = jnp.where(visible, scores.reshape(shape), -1e30)
        highest = jnp.max(jnp.max(scores, axis=0, keepdims=True), axis=2, keepdims=True)
        weights = jnp.where(visible, jnp.exp(scores - highest), 0.0)
        total = jnp.sum(jnp.sum(weights, axis=0, keepdims=True), axis=2, keepdims=True)
        probs_low = (weights / total).reshape(rows, tok_dev).astype(bf16)
        pieces.append(
            lax.dot_general(
                probs_low, values_ref[part], (((0,), (0,)), ((), ())), preferred_element_type=f32
            ).astype(bf16)
        )
    context = pieces[0] if len(pieces) == 1 else jnp.concatenate(pieces, axis=1)
    hidden = residual_ref[...].astype(f32) + context.astype(f32)
    hidden_ref[...] = hidden
    power = jnp.mean(hidden * hidden, axis=1, keepdims=True)
    normed = (hidden * lax.rsqrt(power + 1e-06) * gain_ref[...].astype(f32).reshape(1, -1)).astype(
        bf16
    )
    slots = out_ref.shape[1]
    placing = lax.broadcasted_iota(jnp.int32, (slots, tok_dev), 0) == target_ref[...]
    outgoing = jnp.dot(
        placing.astype(f32).astype(bf16), normed, preferred_element_type=f32
    ).astype(bf16)
    for pipe in range(pipes):
        out_ref[pipe] = outgoing


def backward_kernel(scale, kv_ref, queries_ref, grad_ref, lengths_ref, *refs):
    out_refs, sums_ref = refs[:-1], refs[-1]
    pipes, _, enc_dev, wide = kv_ref.shape
    head, rows = wide // 2, pipes * enc_dev
    f32, bf16 = jnp.float32, jnp.bfloat16
    kv = kv_ref[:, lax.axis_index("expert")].reshape(rows, wide)
    queries, grads = queries_ref[...], grad_ref[...]
    tokens = queries.shape[1]
    keys, values = kv[:, :head], kv[:, head:]
    scores = jnp.dot(keys, queries, preferred_element_type=f32) * scale
    visible = lax.broadcasted_iota(jnp.int32, (rows, tokens), 0) < lengths_ref[...].reshape(1, tokens)
    scores = jnp.where(visible, scores, -1e30)
    highest = jnp.max(scores, axis=0, keepdims=True)
    weights = jnp.where(visible, jnp.exp(scores - highest), 0.0)
    probs = weights / jnp.sum(weights, axis=0, keepdims=True)
    probs_low = probs.astype(bf16)
    grad_probs = jnp.dot(values, grads, preferred_element_type=f32)
    row_delta = jnp.sum(probs * grad_probs, axis=0, keepdims=True)
    grad_scores = (probs * (grad_probs - row_delta) * scale).astype(bf16)
    over_tokens = (((1,), (1,)), ((), ()))
    grad_keys = lax.dot_general(grad_scores, queries, over_tokens, preferred_element_type=f32)
    grad_values = lax.dot_general(probs_low, grads, over_tokens, preferred_element_type=f32)
    sums_ref[...] = jnp.concatenate([grad_keys, grad_values], axis=1).reshape(sums_ref.shape)
    own = lax.axis_index("pipe")
    for s, out_ref in enumerate(out_refs):
        out_ref[...] = sums_ref[lax.rem(own + s, pipes)]


def gradient_kernel(keys_in_ref, values_in_ref, *refs):
    *sum_refs, out_ref = refs
    f32, bf16 = jnp.float32, jnp.bfloat16
    total = sum_refs[0][...]
    for ref in sum_refs[1:]:
        total = total + ref[...]
    total, head = total.astype(bf16), keys_in_ref.shape[0]
    out_ref[...] = jnp.dot(total[:, :head], keys_in_ref[...], preferred_element_type=f32) + jnp.dot(
        total[:, head:], values_in_ref[...], preferred_element_type=f32
    )


def expert_kernel(rows_ref, first_ref, second_ref, out_hbm, out_ref, left):
    chunks = left.shape[0]
    size = rows_ref.shape[0] // chunks
    f32, bf16 = jnp.float32, jnp.bfloat16
    active = jnp.maximum(
        lax.dot_general(
            rows_ref[...], first_ref[...], (((1,), (1,)), ((), ())), preferred_element_type=f32
        ),
        0.0,
    ).astype(bf16)
    leaves = []
    for i in range(chunks):
        chunk = slice(i * size, (i + 1) * size)
        out_ref[chunk] = jnp.dot(
            active[chunk], second_ref[...], preferred_element_type=f32
        ).astype(bf16)
        leaves.append(pltpu.make_async_copy(out_ref.at[chunk], out_hbm.at[chunk], left.at[i]))
        leaves[-1].start()
    for leave in leaves:
        leave.wait()


def combine_kernel(returned_ref, target_ref, hidden_ref, out_ref):
    slots, tok_dev = returned_ref.shape[1], hidden_ref.shape[0]
    f32, bf16 = jnp.float32, jnp.bfloat16
    rows = jnp.sum(returned_ref[...].astype(f32), axis=0).astype(bf16)
    placing = lax.broadcasted_iota(jnp.int32, (slots, tok_dev), 0) == target_ref[...]
    expert_out = lax.dot_general(
        placing.astype(f32).astype(bf16), rows, (((0,), (0,)), ((), ())), preferred_element_type=f32
    )
    out_ref[...] = (hidden_ref[...] + expert_out).astype(bf16)


def per_device(
    enc_states,
    key_weight,
    value_weight,
    queries,
    lengths,
    context_grad,
    residual,
    norm_gain,
    routes,
    w_in,
    w_out,
):
    enc_dev = enc_states.shape[0]
    head = key_weight.shape[1]
    tok_dev = residual.shape[0]
    model = residual.shape[1]
    experts = lax.axis_size("expert")
    pipes = lax.axis_size("pipe")
    cap = tok_dev // (2 * experts)
    scale = 1.0 / math.sqrt(head)
    f32, bf16 = jnp.float32, jnp.bfloat16
    here, own_pipe = lax.axis_index("expert"), lax.axis_index("pipe")
    params = pltpu.CompilerParams(vmem_limit_bytes=(8 << 20) if model <= 1024 else (40 << 20))
    queries_turned = queries.T
    half = (experts // 2, head, tok_dev)
    spread_kv, keep, send, own_lengths, gain, target, near_residual = pl.pallas_call(
        functools.partial(project_kernel, cap),
        out_shape=[
            jax.ShapeDtypeStruct((pipes * experts, enc_dev, 2 * head), bf16),
            jax.ShapeDtypeStruct(half, bf16),
            jax.ShapeDtypeStruct(half, bf16),
            jax.ShapeDtypeStruct((tok_dev,), jnp.int32),
            jax.ShapeDtypeStruct((model,), bf16),
            jax.ShapeDtypeStruct((1, tok_dev), jnp.int32),
            jax.ShapeDtypeStruct((tok_dev, model), bf16),
        ],
        in_specs=[HBM] * 8,
        out_specs=[HBM] + [VMEM] * 6,
        scratch_shapes=[
            pltpu.VMEM((enc_dev, model), bf16),
            pltpu.VMEM((head, model), bf16),
            pltpu.VMEM((head, model), bf16),
            pltpu.VMEM((head, experts * tok_dev), bf16),
            pltpu.VMEM((1, tok_dev), jnp.int32),
            pltpu.VMEM((pipes * experts, enc_dev, 2 * head), bf16),
            pltpu.SemaphoreType.DMA((8,)),
            pltpu.SemaphoreType.DMA,
        ],
        compiler_params=params,
    )(
        *(
            pltpu.with_memory_space_constraint(value, pltpu.HBM)
            for value in (
                enc_states,
                key_weight.T,
                value_weight.T,
                queries_turned,
                lengths,
                norm_gain,
                routes.T,
                residual,
            )
        )
    )
    kv = lax.all_to_all(
        spread_kv, EVERYONE, split_axis=0, concat_axis=0, tiled=True
    ).reshape(pipes, experts, enc_dev, 2 * head)
    chips = experts // 2
    query_blocks = pl.pallas_call(
        gather_kernel,
        out_shape=[jax.ShapeDtypeStruct((2 * head, tok_dev), bf16)] * chips,
        in_specs=[VMEM] * 2,
        out_specs=[VMEM] * chips,
        compiler_params=params,
        cost_estimate=pl.CostEstimate(flops=1 << 34, bytes_accessed=1 << 26, transcendentals=0),
    )(keep, crossed(send, 1))
    query_blocks = [query_blocks[0]] + [crossed(query_blocks[k], 2 * k) for k in range(1, chips)]
    group = max(g for g in range(2, experts + 1, 2) if experts % g == 0 and g * head <= 512)
    blocks = (experts // group, pipes * group * enc_dev, group * head)
    key_blocks, value_blocks = pl.pallas_call(
        functools.partial(block_kernel, group),
        out_shape=[jax.ShapeDtypeStruct(blocks, bf16)] * 2,
        in_specs=[VMEM],
        out_specs=[VMEM] * 2,
        compiler_params=params,
        cost_estimate=pl.CostEstimate(flops=1 << 34, bytes_accessed=1 << 26, transcendentals=0),
    )(kv)
    hidden_state, outgoing = pl.pallas_call(
        functools.partial(attend_kernel, scale, enc_dev, head),
        out_shape=(
            jax.ShapeDtypeStruct((tok_dev, model), f32),
            jax.ShapeDtypeStruct((pipes, experts * cap, model), bf16),
        ),
        in_specs=[VMEM] * (6 + chips),
        out_specs=[VMEM] * 2,
        scratch_shapes=[pltpu.VMEM((model, tok_dev), bf16)],
        compiler_params=params,
    )(key_blocks, value_blocks, own_lengths, near_residual, gain, target, query_blocks[0], *query_blocks[:0:-1])
    outgoing = outgoing.reshape(pipes * experts, cap, model)
    kv, outgoing = lax.optimization_barrier((kv, outgoing))
    total, *others = pl.pallas_call(
        functools.partial(backward_kernel, scale),
        out_shape=[jax.ShapeDtypeStruct((enc_dev, 2 * head), f32)] * pipes,
        in_specs=[VMEM] * 4,
        out_specs=[VMEM] * pipes,
        scratch_shapes=[pltpu.VMEM((pipes, enc_dev, 2 * head), f32)],
        compiler_params=params,
        cost_estimate=pl.CostEstimate(flops=0, bytes_accessed=0, transcendentals=0),
    )(kv, queries_turned, context_grad.T, lengths)
    sums = [total] + [shifted(other, "pipe", s + 1) for s, other in enumerate(others)]
    arrived = lax.all_to_all(outgoing, EVERYONE, split_axis=0, concat_axis=0, tiled=True)
    arrived, *sums = lax.optimization_barrier((arrived, *sums))
    rows = pipes * experts * cap
    part = pl.pallas_call(
        expert_kernel,
        out_shape=jax.ShapeDtypeStruct((rows, model), bf16),
        in_specs=[VMEM] * 3,
        out_specs=HBM,
        scratch_shapes=[pltpu.VMEM((rows, model), bf16), pltpu.SemaphoreType.DMA((2,))],
        compiler_params=params,
        cost_estimate=pl.CostEstimate(
            flops=4 * rows * model * w_in.shape[2], bytes_accessed=1 << 20, transcendentals=0
        ),
    )(arrived.reshape(rows, model), w_in[0].T, w_out[0])
    enc_part = pl.pallas_call(
        gradient_kernel,
        out_shape=jax.ShapeDtypeStruct((enc_dev, model), f32),
        in_specs=[VMEM] * (2 + pipes),
        out_specs=VMEM,
        compiler_params=params,
    )(key_weight.T, value_weight.T, *sums)
    returned = lax.all_to_all(
        part.reshape(pipes * experts, cap, model),
        EVERYONE,
        split_axis=0,
        concat_axis=0,
        tiled=True,
    ).reshape(pipes, experts * cap, model)
    layer_out = pl.pallas_call(
        combine_kernel,
        out_shape=jax.ShapeDtypeStruct((tok_dev, model), bf16),
        in_specs=[VMEM] * 3,
        out_specs=VMEM,
        compiler_params=params,
    )(returned, target, hidden_state)
    for level in range(experts.bit_length() - 1):
        enc_part = enc_part + crossed(enc_part, 1 << level)
    enc_grad = enc_part.astype(bf16)
    return (layer_out, enc_grad)


def solution(mesh):
    placed = (
        P("pipe", None),
        P(None, "expert"),
        P(None, "expert"),
        P("pipe", "expert"),
        P("pipe"),
        P("pipe", "expert"),
        P(("pipe", "expert"), None),
        P(),
        P(("pipe", "expert"), None),
        P("expert", None, "pipe"),
        P("expert", "pipe", None),
    )
    return jax.shard_map(
        per_device,
        mesh=mesh,
        in_specs=placed,
        out_specs=(P(("pipe", "expert"), None), P("pipe", None)),
        check_vma=False,
    )
```

```python
import functools
import math

import jax
import jax.numpy as jnp
from jax import lax
from jax.experimental import pallas as pl
from jax.experimental.pallas import tpu as pltpu
from jax.sharding import PartitionSpec as P

EVERYONE = ("pipe", "expert")
VMEM = pl.BlockSpec(memory_space=pltpu.VMEM)
HBM = pl.BlockSpec(memory_space=pltpu.HBM)


def shifted(value, axis, step):
    size = lax.axis_size(axis)
    return lax.ppermute(value, axis, [(i, (i + step) % size) for i in range(size)])


def crossed(value, bit):
    size = lax.axis_size("expert")
    return lax.ppermute(value, "expert", [(i, i ^ bit) for i in range(size)])


def project_kernel(
    cap, enc_hbm, key_hbm, value_hbm, queries_hbm, lengths_hbm, gain_hbm, routes_hbm, residual_hbm, *refs
):
    spread_hbm, keep_ref, send_ref, lengths_ref, gain_ref, target_ref, residual_ref = refs[:7]
    enc_ref, key_ref, value_ref, queries_ref, routes_ref, spread_ref, arrived, left = refs[7:]
    f32, bf16 = jnp.float32, jnp.bfloat16
    here, experts = lax.axis_index("expert"), lax.axis_size("expert")
    tok_dev = routes_ref.shape[1]
    own_tokens = pl.ds(pl.multiple_of(here * tok_dev, tok_dev), tok_dev)
    fetches = [
        pltpu.make_async_copy(source, target, arrived.at[i])
        for i, (source, target) in enumerate(
            (
                (enc_hbm, enc_ref),
                (key_hbm, key_ref),
                (value_hbm, value_ref),
                (routes_hbm, routes_ref),
                (queries_hbm, queries_ref),
                (lengths_hbm.at[own_tokens], lengths_ref),
                (gain_hbm, gain_ref),
                (residual_hbm, residual_ref),
            )
        )
    ]
    for fetch in fetches:
        fetch.start()
    for fetch in fetches[:3]:
        fetch.wait()
    enc = enc_ref[...]
    own = jnp.concatenate(
        [
            lax.dot_general(enc, ref[...], (((1,), (1,)), ((), ())), preferred_element_type=f32)
            for ref in (key_ref, value_ref)
        ],
        axis=1,
    )
    spread_ref[...] = jnp.broadcast_to(own.astype(bf16)[None], spread_ref.shape)
    leave = pltpu.make_async_copy(spread_ref, spread_hbm, left)
    leave.start()
    for fetch in fetches[3:]:
        fetch.wait()
    core = lax.rem(here, 2)
    for chip in range(experts // 2):
        for ref, which in ((keep_ref, core), (send_ref, 1 - core)):
            lanes = pl.ds(pl.multiple_of((2 * chip + which) * tok_dev, tok_dev), tok_dev)
            ref[chip] = queries_ref[:, lanes]
    target_ref[...] = routes_ref[...]
    leave.wait()


def gather_kernel(cap, keep_ref, got_ref, routes_ref, target_ref, *out_refs):
    f32, bf16 = jnp.float32, jnp.bfloat16
    experts, tok_dev = lax.axis_size("expert"), routes_ref.shape[1]
    chip = lax.axis_index("expert") // 2
    head = keep_ref.shape[1]
    for k, out_ref in enumerate(out_refs):
        out_ref[:head] = keep_ref[lax.bitwise_xor(chip, k)]
        out_ref[head:] = got_ref[lax.bitwise_xor(chip, k)]
    routes = routes_ref[...]
    onehot = lax.broadcasted_iota(jnp.int32, (experts, tok_dev), 0) == routes
    earlier = lax.broadcasted_iota(jnp.int32, (tok_dev, tok_dev), 0) < lax.broadcasted_iota(
        jnp.int32, (tok_dev, tok_dev), 1
    )
    before = jnp.dot(
        onehot.astype(f32).astype(bf16), earlier.astype(f32).astype(bf16), preferred_element_type=f32
    )
    slot_rank = jnp.sum(jnp.where(onehot, before, 0.0), axis=0, keepdims=True).astype(jnp.int32)
    target_ref[...] = jnp.where(slot_rank < cap, routes * cap + slot_rank, -1)


def block_kernel(group, kv_ref, keys_ref, values_ref):
    pipes, heads, enc_dev, wide = kv_ref.shape
    head = wide // 2
    rows, cols = pipes * group * enc_dev, group * head
    f32, bf16 = jnp.float32, jnp.bfloat16
    row_head = lax.rem(lax.broadcasted_iota(jnp.int32, (rows, cols), 0) // enc_dev, group)
    same_head = row_head == lax.broadcasted_iota(jnp.int32, (rows, cols), 1) // head
    left = lax.broadcasted_iota(jnp.int32, (rows, wide), 1) < head
    for part in range(heads // group):
        kv = kv_ref[:, part * group : (part + 1) * group].reshape(rows, wide).astype(f32)
        turned = pltpu.roll(kv, head, 1)
        twice_keys = jnp.where(left, kv, turned).astype(bf16)
        twice_values = jnp.where(left, turned, kv).astype(bf16)
        for twice, ref in ((twice_keys, keys_ref), (twice_values, values_ref)):
            block = jnp.concatenate([twice] * (group // 2), axis=1)
            ref[part] = jnp.where(same_head, block, jnp.zeros_like(block))


def attend_kernel(
    scale, enc_dev, head, keys_ref, values_ref, lengths_ref, residual_ref, gain_ref, target_ref, *refs
):
    parts, rows, cols = keys_ref.shape
    group, heads = cols // head, parts * cols // head
    *query_refs, hidden_ref, out_ref, q_ref = refs
    pipes, tok_dev = rows // (group * enc_dev), q_ref.shape[1]
    f32, bf16 = jnp.float32, jnp.bfloat16
    here = lax.axis_index("expert")
    for k, ref in zip((0, *range(len(query_refs) - 1, 0, -1)), query_refs, strict=True):
        for i in range(2):
            which = pl.multiple_of(lax.bitwise_xor(here, 2 * k + i) * head, head)
            q_ref[pl.ds(which, head)] = ref[i * head : (i + 1) * head]
    shape = (pipes, group, enc_dev, tok_dev)
    position = lax.broadcasted_iota(jnp.int32, shape, 0) * enc_dev + lax.broadcasted_iota(
        jnp.int32, shape, 2
    )
    visible = position < lengths_ref[...].reshape(1, 1, 1, tok_dev)
    pieces = []
    for part in range(parts):
        scores = scale * jnp.dot(
            keys_ref[part], q_ref[part * cols : (part + 1) * cols], preferred_element_type=f32
        )
        scores = jnp.where(visible, scores.reshape(shape), -1e30)
        highest = jnp.max(jnp.max(scores, axis=0, keepdims=True), axis=2, keepdims=True)
        weights = jnp.where(visible, jnp.exp(scores - highest), 0.0)
        total = jnp.sum(jnp.sum(weights, axis=0, keepdims=True), axis=2, keepdims=True)
        probs_low = (weights / total).reshape(rows, tok_dev).astype(bf16)
        pieces.append(
            lax.dot_general(
                probs_low, values_ref[part], (((0,), (0,)), ((), ())), preferred_element_type=f32
            ).astype(bf16)
        )
    context = pieces[0] if len(pieces) == 1 else jnp.concatenate(pieces, axis=1)
    hidden = residual_ref[...].astype(f32) + context.astype(f32)
    hidden_ref[...] = hidden
    power = jnp.mean(hidden * hidden, axis=1, keepdims=True)
    normed = (hidden * lax.rsqrt(power + 1e-06) * gain_ref[...].astype(f32).reshape(1, -1)).astype(
        bf16
    )
    slots = out_ref.shape[1]
    placing = lax.broadcasted_iota(jnp.int32, (slots, tok_dev), 0) == target_ref[...]
    outgoing = jnp.dot(
        placing.astype(f32).astype(bf16), normed, preferred_element_type=f32
    ).astype(bf16)
    for pipe in range(pipes):
        out_ref[pipe] = outgoing


def backward_kernel(scale, kv_ref, queries_ref, grad_ref, lengths_ref, *refs):
    out_refs, sums_ref = refs[:-1], refs[-1]
    pipes, _, enc_dev, wide = kv_ref.shape
    head, rows = wide // 2, pipes * enc_dev
    f32, bf16 = jnp.float32, jnp.bfloat16
    kv = kv_ref[:, lax.axis_index("expert")].reshape(rows, wide)
    queries, grads = queries_ref[...], grad_ref[...]
    tokens = queries.shape[1]
    keys, values = kv[:, :head], kv[:, head:]
    scores = jnp.dot(keys, queries, preferred_element_type=f32) * scale
    visible = lax.broadcasted_iota(jnp.int32, (rows, tokens), 0) < lengths_ref[...].reshape(1, tokens)
    scores = jnp.where(visible, scores, -1e30)
    highest = jnp.max(scores, axis=0, keepdims=True)
    weights = jnp.where(visible, jnp.exp(scores - highest), 0.0)
    probs = weights / jnp.sum(weights, axis=0, keepdims=True)
    probs_low = probs.astype(bf16)
    grad_probs = jnp.dot(values, grads, preferred_element_type=f32)
    row_delta = jnp.sum(probs * grad_probs, axis=0, keepdims=True)
    grad_scores = (probs * (grad_probs - row_delta) * scale).astype(bf16)
    over_tokens = (((1,), (1,)), ((), ()))
    grad_keys = lax.dot_general(grad_scores, queries, over_tokens, preferred_element_type=f32)
    grad_values = lax.dot_general(probs_low, grads, over_tokens, preferred_element_type=f32)
    sums_ref[...] = jnp.concatenate([grad_keys, grad_values], axis=1).reshape(sums_ref.shape)
    own = lax.axis_index("pipe")
    for s, out_ref in enumerate(out_refs):
        out_ref[...] = sums_ref[lax.rem(own + s, pipes)]


def gradient_kernel(keys_in_ref, values_in_ref, *refs):
    *sum_refs, out_ref = refs
    f32, bf16 = jnp.float32, jnp.bfloat16
    total = sum_refs[0][...]
    for ref in sum_refs[1:]:
        total = total + ref[...]
    total, head = total.astype(bf16), keys_in_ref.shape[0]
    out_ref[...] = jnp.dot(total[:, :head], keys_in_ref[...], preferred_element_type=f32) + jnp.dot(
        total[:, head:], values_in_ref[...], preferred_element_type=f32
    )


def expert_kernel(rows_ref, first_ref, second_ref, out_hbm, out_ref, left):
    chunks = left.shape[0]
    size = rows_ref.shape[0] // chunks
    f32, bf16 = jnp.float32, jnp.bfloat16
    active = jnp.maximum(
        lax.dot_general(
            rows_ref[...], first_ref[...], (((1,), (1,)), ((), ())), preferred_element_type=f32
        ),
        0.0,
    ).astype(bf16)
    leaves = []
    for i in range(chunks):
        chunk = slice(i * size, (i + 1) * size)
        out_ref[chunk] = jnp.dot(
            active[chunk], second_ref[...], preferred_element_type=f32
        ).astype(bf16)
        leaves.append(pltpu.make_async_copy(out_ref.at[chunk], out_hbm.at[chunk], left.at[i]))
        leaves[-1].start()
    for leave in leaves:
        leave.wait()


def combine_kernel(returned_ref, target_ref, hidden_ref, out_ref):
    slots, tok_dev = returned_ref.shape[1], hidden_ref.shape[0]
    f32, bf16 = jnp.float32, jnp.bfloat16
    rows = jnp.sum(returned_ref[...].astype(f32), axis=0).astype(bf16)
    placing = lax.broadcasted_iota(jnp.int32, (slots, tok_dev), 0) == target_ref[...]
    expert_out = lax.dot_general(
        placing.astype(f32).astype(bf16), rows, (((0,), (0,)), ((), ())), preferred_element_type=f32
    )
    out_ref[...] = (hidden_ref[...] + expert_out).astype(bf16)


def per_device(
    enc_states,
    key_weight,
    value_weight,
    queries,
    lengths,
    context_grad,
    residual,
    norm_gain,
    routes,
    w_in,
    w_out,
):
    enc_dev = enc_states.shape[0]
    head = key_weight.shape[1]
    tok_dev = residual.shape[0]
    model = residual.shape[1]
    experts = lax.axis_size("expert")
    pipes = lax.axis_size("pipe")
    cap = tok_dev // (2 * experts)
    scale = 1.0 / math.sqrt(head)
    f32, bf16 = jnp.float32, jnp.bfloat16
    here, own_pipe = lax.axis_index("expert"), lax.axis_index("pipe")
    params = pltpu.CompilerParams(vmem_limit_bytes=(8 << 20) if model <= 1024 else (40 << 20))
    queries_turned = queries.T
    half = (experts // 2, head, tok_dev)
    spread_kv, keep, send, own_lengths, gain, target, near_residual = pl.pallas_call(
        functools.partial(project_kernel, cap),
        out_shape=[
            jax.ShapeDtypeStruct((pipes * experts, enc_dev, 2 * head), bf16),
            jax.ShapeDtypeStruct(half, bf16),
            jax.ShapeDtypeStruct(half, bf16),
            jax.ShapeDtypeStruct((tok_dev,), jnp.int32),
            jax.ShapeDtypeStruct((model,), bf16),
            jax.ShapeDtypeStruct((1, tok_dev), jnp.int32),
            jax.ShapeDtypeStruct((tok_dev, model), bf16),
        ],
        in_specs=[HBM] * 8,
        out_specs=[HBM] + [VMEM] * 6,
        scratch_shapes=[
            pltpu.VMEM((enc_dev, model), bf16),
            pltpu.VMEM((head, model), bf16),
            pltpu.VMEM((head, model), bf16),
            pltpu.VMEM((head, experts * tok_dev), bf16),
            pltpu.VMEM((1, tok_dev), jnp.int32),
            pltpu.VMEM((pipes * experts, enc_dev, 2 * head), bf16),
            pltpu.SemaphoreType.DMA((8,)),
            pltpu.SemaphoreType.DMA,
        ],
        compiler_params=params,
    )(
        *(
            pltpu.with_memory_space_constraint(value, pltpu.HBM)
            for value in (
                enc_states,
                key_weight.T,
                value_weight.T,
                queries_turned,
                lengths,
                norm_gain,
                routes.T,
                residual,
            )
        )
    )
    kv = lax.all_to_all(
        spread_kv, EVERYONE, split_axis=0, concat_axis=0, tiled=True
    ).reshape(pipes, experts, enc_dev, 2 * head)
    chips = experts // 2
    target, *query_blocks = pl.pallas_call(
        functools.partial(gather_kernel, cap),
        out_shape=[jax.ShapeDtypeStruct((1, tok_dev), jnp.int32)]
        + [jax.ShapeDtypeStruct((2 * head, tok_dev), bf16)] * chips,
        in_specs=[VMEM] * 3,
        out_specs=[VMEM] * (1 + chips),
        compiler_params=params,
        cost_estimate=pl.CostEstimate(flops=1 << 34, bytes_accessed=1 << 26, transcendentals=0),
    )(keep, crossed(send, 1), target)
    query_blocks = [query_blocks[0]] + [crossed(query_blocks[k], 2 * k) for k in range(1, chips)]
    group = max(g for g in range(2, experts + 1, 2) if experts % g == 0 and g * head <= 512)
    blocks = (experts // group, pipes * group * enc_dev, group * head)
    key_blocks, value_blocks = pl.pallas_call(
        functools.partial(block_kernel, group),
        out_shape=[jax.ShapeDtypeStruct(blocks, bf16)] * 2,
        in_specs=[VMEM],
        out_specs=[VMEM] * 2,
        compiler_params=params,
        cost_estimate=pl.CostEstimate(flops=1 << 34, bytes_accessed=1 << 26, transcendentals=0),
    )(kv)
    hidden_state, outgoing = pl.pallas_call(
        functools.partial(attend_kernel, scale, enc_dev, head),
        out_shape=(
            jax.ShapeDtypeStruct((tok_dev, model), f32),
            jax.ShapeDtypeStruct((pipes, experts * cap, model), bf16),
        ),
        in_specs=[VMEM] * (6 + chips),
        out_specs=[VMEM] * 2,
        scratch_shapes=[pltpu.VMEM((model, tok_dev), bf16)],
        compiler_params=params,
    )(key_blocks, value_blocks, own_lengths, near_residual, gain, target, query_blocks[0], *query_blocks[:0:-1])
    outgoing = outgoing.reshape(pipes * experts, cap, model)
    kv, outgoing = lax.optimization_barrier((kv, outgoing))
    total, *others = pl.pallas_call(
        functools.partial(backward_kernel, scale),
        out_shape=[jax.ShapeDtypeStruct((enc_dev, 2 * head), f32)] * pipes,
        in_specs=[VMEM] * 4,
        out_specs=[VMEM] * pipes,
        scratch_shapes=[pltpu.VMEM((pipes, enc_dev, 2 * head), f32)],
        compiler_params=params,
        cost_estimate=pl.CostEstimate(flops=0, bytes_accessed=0, transcendentals=0),
    )(kv, queries_turned, context_grad.T, lengths)
    sums = [total] + [shifted(other, "pipe", s + 1) for s, other in enumerate(others)]
    arrived = lax.all_to_all(outgoing, EVERYONE, split_axis=0, concat_axis=0, tiled=True)
    arrived, *sums = lax.optimization_barrier((arrived, *sums))
    rows = pipes * experts * cap
    part = pl.pallas_call(
        expert_kernel,
        out_shape=jax.ShapeDtypeStruct((rows, model), bf16),
        in_specs=[VMEM] * 3,
        out_specs=HBM,
        scratch_shapes=[pltpu.VMEM((rows, model), bf16), pltpu.SemaphoreType.DMA((2,))],
        compiler_params=params,
        cost_estimate=pl.CostEstimate(
            flops=4 * rows * model * w_in.shape[2], bytes_accessed=1 << 20, transcendentals=0
        ),
    )(arrived.reshape(rows, model), w_in[0].T, w_out[0])
    enc_part = pl.pallas_call(
        gradient_kernel,
        out_shape=jax.ShapeDtypeStruct((enc_dev, model), f32),
        in_specs=[VMEM] * (2 + pipes),
        out_specs=VMEM,
        compiler_params=params,
    )(key_weight.T, value_weight.T, *sums)
    returned = lax.all_to_all(
        part.reshape(pipes * experts, cap, model),
        EVERYONE,
        split_axis=0,
        concat_axis=0,
        tiled=True,
    ).reshape(pipes, experts * cap, model)
    layer_out = pl.pallas_call(
        combine_kernel,
        out_shape=jax.ShapeDtypeStruct((tok_dev, model), bf16),
        in_specs=[VMEM] * 3,
        out_specs=VMEM,
        compiler_params=params,
    )(returned, target, hidden_state)
    for level in range(experts.bit_length() - 1):
        enc_part = enc_part + crossed(enc_part, 1 << level)
    enc_grad = enc_part.astype(bf16)
    return (layer_out, enc_grad)


def solution(mesh):
    placed = (
        P("pipe", None),
        P(None, "expert"),
        P(None, "expert"),
        P("pipe", "expert"),
        P("pipe"),
        P("pipe", "expert"),
        P(("pipe", "expert"), None),
        P(),
        P(("pipe", "expert"), None),
        P("expert", None, "pipe"),
        P("expert", "pipe", None),
    )
    return jax.shard_map(
        per_device,
        mesh=mesh,
        in_specs=placed,
        out_specs=(P(("pipe", "expert"), None), P("pipe", None)),
        check_vma=False,
    )
```

```python
import functools
import math

import jax
import jax.numpy as jnp
from jax import lax
from jax.experimental import pallas as pl
from jax.experimental.pallas import tpu as pltpu
from jax.sharding import PartitionSpec as P

EVERYONE = ("pipe", "expert")
VMEM = pl.BlockSpec(memory_space=pltpu.VMEM)
HBM = pl.BlockSpec(memory_space=pltpu.HBM)


def shifted(value, axis, step):
    size = lax.axis_size(axis)
    return lax.ppermute(value, axis, [(i, (i + step) % size) for i in range(size)])


def crossed(value, bit):
    size = lax.axis_size("expert")
    return lax.ppermute(value, "expert", [(i, i ^ bit) for i in range(size)])


def project_kernel(
    cap, enc_hbm, key_hbm, value_hbm, queries_hbm, lengths_hbm, gain_hbm, routes_hbm, residual_hbm, *refs
):
    spread_hbm, keep_ref, send_ref, lengths_ref, gain_ref, target_ref, residual_ref = refs[:7]
    enc_ref, key_ref, value_ref, queries_ref, routes_ref, spread_ref, arrived, left = refs[7:]
    f32, bf16 = jnp.float32, jnp.bfloat16
    here, experts = lax.axis_index("expert"), lax.axis_size("expert")
    tok_dev = routes_ref.shape[1]
    own_tokens = pl.ds(pl.multiple_of(here * tok_dev, tok_dev), tok_dev)
    fetches = [
        pltpu.make_async_copy(source, target, arrived.at[i])
        for i, (source, target) in enumerate(
            (
                (enc_hbm, enc_ref),
                (key_hbm, key_ref),
                (value_hbm, value_ref),
                (routes_hbm, routes_ref),
                (queries_hbm, queries_ref),
                (lengths_hbm.at[own_tokens], lengths_ref),
                (gain_hbm, gain_ref),
                (residual_hbm, residual_ref),
            )
        )
    ]
    for fetch in fetches:
        fetch.start()
    for fetch in fetches[:3]:
        fetch.wait()
    enc = enc_ref[...]
    own = jnp.concatenate(
        [
            lax.dot_general(enc, ref[...], (((1,), (1,)), ((), ())), preferred_element_type=f32)
            for ref in (key_ref, value_ref)
        ],
        axis=1,
    )
    spread_ref[...] = jnp.broadcast_to(own.astype(bf16)[None], spread_ref.shape)
    leave = pltpu.make_async_copy(spread_ref, spread_hbm, left)
    leave.start()
    for fetch in fetches[3:]:
        fetch.wait()
    core = lax.rem(here, 2)
    for chip in range(experts // 2):
        for ref, which in ((keep_ref, core), (send_ref, 1 - core)):
            lanes = pl.ds(pl.multiple_of((2 * chip + which) * tok_dev, tok_dev), tok_dev)
            ref[chip] = queries_ref[:, lanes]
    routes = routes_ref[...]
    onehot = lax.broadcasted_iota(jnp.int32, (experts, tok_dev), 0) == routes
    earlier = lax.broadcasted_iota(jnp.int32, (tok_dev, tok_dev), 0) < lax.broadcasted_iota(
        jnp.int32, (tok_dev, tok_dev), 1
    )
    before = jnp.dot(
        onehot.astype(f32).astype(bf16), earlier.astype(f32).astype(bf16), preferred_element_type=f32
    )
    slot_rank = jnp.sum(jnp.where(onehot, before, 0.0), axis=0, keepdims=True).astype(jnp.int32)
    target_ref[...] = jnp.where(slot_rank < cap, routes * cap + slot_rank, -1)
    leave.wait()


def gather_kernel(keep_ref, got_ref, *out_refs):
    chip = lax.axis_index("expert") // 2
    head = keep_ref.shape[1]
    for k, out_ref in enumerate(out_refs):
        out_ref[:head] = keep_ref[lax.bitwise_xor(chip, k)]
        out_ref[head:] = got_ref[lax.bitwise_xor(chip, k)]


def block_kernel(group, kv_ref, keys_ref, values_ref):
    pipes, heads, enc_dev, wide = kv_ref.shape
    head = wide // 2
    rows, cols = pipes * group * enc_dev, group * head
    f32, bf16 = jnp.float32, jnp.bfloat16
    row_head = lax.rem(lax.broadcasted_iota(jnp.int32, (rows, cols), 0) // enc_dev, group)
    same_head = row_head == lax.broadcasted_iota(jnp.int32, (rows, cols), 1) // head
    left = lax.broadcasted_iota(jnp.int32, (rows, wide), 1) < head
    for part in range(heads // group):
        kv = kv_ref[:, part * group : (part + 1) * group].reshape(rows, wide).astype(f32)
        turned = pltpu.roll(kv, head, 1)
        twice_keys = jnp.where(left, kv, turned).astype(bf16)
        twice_values = jnp.where(left, turned, kv).astype(bf16)
        for twice, ref in ((twice_keys, keys_ref), (twice_values, values_ref)):
            block = jnp.concatenate([twice] * (group // 2), axis=1)
            ref[part] = jnp.where(same_head, block, jnp.zeros_like(block))


def attend_kernel(
    scale, enc_dev, head, keys_ref, values_ref, lengths_ref, residual_ref, gain_ref, target_ref, *refs
):
    parts, rows, cols = keys_ref.shape
    group, heads = cols // head, parts * cols // head
    *query_refs, hidden_ref, out_ref, q_ref = refs
    pipes, tok_dev = rows // (group * enc_dev), q_ref.shape[1]
    f32, bf16 = jnp.float32, jnp.bfloat16
    here = lax.axis_index("expert")
    for k, ref in zip((0, len(query_refs) - 1, *range(1, len(query_refs) - 1)), query_refs, strict=True):
        for i in range(2):
            which = pl.multiple_of(lax.bitwise_xor(here, 2 * k + i) * head, head)
            q_ref[pl.ds(which, head)] = ref[i * head : (i + 1) * head]
    shape = (pipes, group, enc_dev, tok_dev)
    position = lax.broadcasted_iota(jnp.int32, shape, 0) * enc_dev + lax.broadcasted_iota(
        jnp.int32, shape, 2
    )
    visible = position < lengths_ref[...].reshape(1, 1, 1, tok_dev)
    pieces = []
    for part in range(parts):
        scores = scale * jnp.dot(
            keys_ref[part], q_ref[part * cols : (part + 1) * cols], preferred_element_type=f32
        )
        scores = jnp.where(visible, scores.reshape(shape), -1e30)
        highest = jnp.max(jnp.max(scores, axis=0, keepdims=True), axis=2, keepdims=True)
        weights = jnp.where(visible, jnp.exp(scores - highest), 0.0)
        total = jnp.sum(jnp.sum(weights, axis=0, keepdims=True), axis=2, keepdims=True)
        probs_low = (weights / total).reshape(rows, tok_dev).astype(bf16)
        pieces.append(
            lax.dot_general(
                probs_low, values_ref[part], (((0,), (0,)), ((), ())), preferred_element_type=f32
            ).astype(bf16)
        )
    context = pieces[0] if len(pieces) == 1 else jnp.concatenate(pieces, axis=1)
    hidden = residual_ref[...].astype(f32) + context.astype(f32)
    hidden_ref[...] = hidden
    power = jnp.mean(hidden * hidden, axis=1, keepdims=True)
    normed = (hidden * lax.rsqrt(power + 1e-06) * gain_ref[...].astype(f32).reshape(1, -1)).astype(
        bf16
    )
    slots = out_ref.shape[1]
    placing = lax.broadcasted_iota(jnp.int32, (slots, tok_dev), 0) == target_ref[...]
    outgoing = jnp.dot(
        placing.astype(f32).astype(bf16), normed, preferred_element_type=f32
    ).astype(bf16)
    for pipe in range(pipes):
        out_ref[pipe] = outgoing


def backward_kernel(scale, kv_ref, queries_ref, grad_ref, lengths_ref, *refs):
    out_refs, sums_ref = refs[:-1], refs[-1]
    pipes, _, enc_dev, wide = kv_ref.shape
    head, rows = wide // 2, pipes * enc_dev
    f32, bf16 = jnp.float32, jnp.bfloat16
    kv = kv_ref[:, lax.axis_index("expert")].reshape(rows, wide)
    queries, grads = queries_ref[...], grad_ref[...]
    tokens = queries.shape[1]
    keys, values = kv[:, :head], kv[:, head:]
    scores = jnp.dot(keys, queries, preferred_element_type=f32) * scale
    visible = lax.broadcasted_iota(jnp.int32, (rows, tokens), 0) < lengths_ref[...].reshape(1, tokens)
    scores = jnp.where(visible, scores, -1e30)
    highest = jnp.max(scores, axis=0, keepdims=True)
    weights = jnp.where(visible, jnp.exp(scores - highest), 0.0)
    probs = weights / jnp.sum(weights, axis=0, keepdims=True)
    probs_low = probs.astype(bf16)
    grad_probs = jnp.dot(values, grads, preferred_element_type=f32)
    row_delta = jnp.sum(probs * grad_probs, axis=0, keepdims=True)
    grad_scores = (probs * (grad_probs - row_delta) * scale).astype(bf16)
    over_tokens = (((1,), (1,)), ((), ()))
    grad_keys = lax.dot_general(grad_scores, queries, over_tokens, preferred_element_type=f32)
    grad_values = lax.dot_general(probs_low, grads, over_tokens, preferred_element_type=f32)
    sums_ref[...] = jnp.concatenate([grad_keys, grad_values], axis=1).reshape(sums_ref.shape)
    own = lax.axis_index("pipe")
    for s, out_ref in enumerate(out_refs):
        out_ref[...] = sums_ref[lax.rem(own + s, pipes)]


def gradient_kernel(keys_in_ref, values_in_ref, *refs):
    *sum_refs, out_ref = refs
    f32, bf16 = jnp.float32, jnp.bfloat16
    total = sum_refs[0][...]
    for ref in sum_refs[1:]:
        total = total + ref[...]
    total, head = total.astype(bf16), keys_in_ref.shape[0]
    out_ref[...] = jnp.dot(total[:, :head], keys_in_ref[...], preferred_element_type=f32) + jnp.dot(
        total[:, head:], values_in_ref[...], preferred_element_type=f32
    )


def expert_kernel(rows_ref, first_ref, second_ref, out_hbm, out_ref, left):
    chunks = left.shape[0]
    size = rows_ref.shape[0] // chunks
    f32, bf16 = jnp.float32, jnp.bfloat16
    active = jnp.maximum(
        lax.dot_general(
            rows_ref[...], first_ref[...], (((1,), (1,)), ((), ())), preferred_element_type=f32
        ),
        0.0,
    ).astype(bf16)
    leaves = []
    for i in range(chunks):
        chunk = slice(i * size, (i + 1) * size)
        out_ref[chunk] = jnp.dot(
            active[chunk], second_ref[...], preferred_element_type=f32
        ).astype(bf16)
        leaves.append(pltpu.make_async_copy(out_ref.at[chunk], out_hbm.at[chunk], left.at[i]))
        leaves[-1].start()
    for leave in leaves:
        leave.wait()


def combine_kernel(returned_ref, target_ref, hidden_ref, out_ref):
    slots, tok_dev = returned_ref.shape[1], hidden_ref.shape[0]
    f32, bf16 = jnp.float32, jnp.bfloat16
    rows = jnp.sum(returned_ref[...].astype(f32), axis=0).astype(bf16)
    placing = lax.broadcasted_iota(jnp.int32, (slots, tok_dev), 0) == target_ref[...]
    expert_out = lax.dot_general(
        placing.astype(f32).astype(bf16), rows, (((0,), (0,)), ((), ())), preferred_element_type=f32
    )
    out_ref[...] = (hidden_ref[...] + expert_out).astype(bf16)


def per_device(
    enc_states,
    key_weight,
    value_weight,
    queries,
    lengths,
    context_grad,
    residual,
    norm_gain,
    routes,
    w_in,
    w_out,
):
    enc_dev = enc_states.shape[0]
    head = key_weight.shape[1]
    tok_dev = residual.shape[0]
    model = residual.shape[1]
    experts = lax.axis_size("expert")
    pipes = lax.axis_size("pipe")
    cap = tok_dev // (2 * experts)
    scale = 1.0 / math.sqrt(head)
    f32, bf16 = jnp.float32, jnp.bfloat16
    here, own_pipe = lax.axis_index("expert"), lax.axis_index("pipe")
    params = pltpu.CompilerParams(vmem_limit_bytes=(8 << 20) if model <= 1024 else (40 << 20))
    queries_turned = queries.T
    half = (experts // 2, head, tok_dev)
    spread_kv, keep, send, own_lengths, gain, target, near_residual = pl.pallas_call(
        functools.partial(project_kernel, cap),
        out_shape=[
            jax.ShapeDtypeStruct((pipes * experts, enc_dev, 2 * head), bf16),
            jax.ShapeDtypeStruct(half, bf16),
            jax.ShapeDtypeStruct(half, bf16),
            jax.ShapeDtypeStruct((tok_dev,), jnp.int32),
            jax.ShapeDtypeStruct((model,), bf16),
            jax.ShapeDtypeStruct((1, tok_dev), jnp.int32),
            jax.ShapeDtypeStruct((tok_dev, model), bf16),
        ],
        in_specs=[HBM] * 8,
        out_specs=[HBM] + [VMEM] * 6,
        scratch_shapes=[
            pltpu.VMEM((enc_dev, model), bf16),
            pltpu.VMEM((head, model), bf16),
            pltpu.VMEM((head, model), bf16),
            pltpu.VMEM((head, experts * tok_dev), bf16),
            pltpu.VMEM((1, tok_dev), jnp.int32),
            pltpu.VMEM((pipes * experts, enc_dev, 2 * head), bf16),
            pltpu.SemaphoreType.DMA((8,)),
            pltpu.SemaphoreType.DMA,
        ],
        compiler_params=params,
    )(
        *(
            pltpu.with_memory_space_constraint(value, pltpu.HBM)
            for value in (
                enc_states,
                key_weight.T,
                value_weight.T,
                queries_turned,
                lengths,
                norm_gain,
                routes.T,
                residual,
            )
        )
    )
    kv = lax.all_to_all(
        spread_kv, EVERYONE, split_axis=0, concat_axis=0, tiled=True
    ).reshape(pipes, experts, enc_dev, 2 * head)
    chips = experts // 2
    query_blocks = pl.pallas_call(
        gather_kernel,
        out_shape=[jax.ShapeDtypeStruct((2 * head, tok_dev), bf16)] * chips,
        in_specs=[VMEM] * 2,
        out_specs=[VMEM] * chips,
        compiler_params=params,
        cost_estimate=pl.CostEstimate(flops=1 << 34, bytes_accessed=1 << 26, transcendentals=0),
    )(keep, crossed(send, 1))
    query_blocks = [query_blocks[0]] + [crossed(query_blocks[k], 2 * k) for k in range(1, chips)]
    group = max(g for g in range(2, experts + 1, 2) if experts % g == 0 and g * head <= 512)
    blocks = (experts // group, pipes * group * enc_dev, group * head)
    key_blocks, value_blocks = pl.pallas_call(
        functools.partial(block_kernel, group),
        out_shape=[jax.ShapeDtypeStruct(blocks, bf16)] * 2,
        in_specs=[VMEM],
        out_specs=[VMEM] * 2,
        compiler_params=params,
        cost_estimate=pl.CostEstimate(flops=1 << 34, bytes_accessed=1 << 26, transcendentals=0),
    )(kv)
    hidden_state, outgoing = pl.pallas_call(
        functools.partial(attend_kernel, scale, enc_dev, head),
        out_shape=(
            jax.ShapeDtypeStruct((tok_dev, model), f32),
            jax.ShapeDtypeStruct((pipes, experts * cap, model), bf16),
        ),
        in_specs=[VMEM] * (6 + chips),
        out_specs=[VMEM] * 2,
        scratch_shapes=[pltpu.VMEM((model, tok_dev), bf16)],
        compiler_params=params,
    )(key_blocks, value_blocks, own_lengths, near_residual, gain, target, query_blocks[0], query_blocks[-1], *query_blocks[1:-1])
    outgoing = outgoing.reshape(pipes * experts, cap, model)
    kv, outgoing = lax.optimization_barrier((kv, outgoing))
    total, *others = pl.pallas_call(
        functools.partial(backward_kernel, scale),
        out_shape=[jax.ShapeDtypeStruct((enc_dev, 2 * head), f32)] * pipes,
        in_specs=[VMEM] * 4,
        out_specs=[VMEM] * pipes,
        scratch_shapes=[pltpu.VMEM((pipes, enc_dev, 2 * head), f32)],
        compiler_params=params,
        cost_estimate=pl.CostEstimate(flops=0, bytes_accessed=0, transcendentals=0),
    )(kv, queries_turned, context_grad.T, lengths)
    sums = [total] + [shifted(other, "pipe", s + 1) for s, other in enumerate(others)]
    arrived = lax.all_to_all(outgoing, EVERYONE, split_axis=0, concat_axis=0, tiled=True)
    arrived, *sums = lax.optimization_barrier((arrived, *sums))
    rows = pipes * experts * cap
    part = pl.pallas_call(
        expert_kernel,
        out_shape=jax.ShapeDtypeStruct((rows, model), bf16),
        in_specs=[VMEM] * 3,
        out_specs=HBM,
        scratch_shapes=[pltpu.VMEM((rows, model), bf16), pltpu.SemaphoreType.DMA((2,))],
        compiler_params=params,
        cost_estimate=pl.CostEstimate(
            flops=4 * rows * model * w_in.shape[2], bytes_accessed=1 << 20, transcendentals=0
        ),
    )(arrived.reshape(rows, model), w_in[0].T, w_out[0])
    enc_part = pl.pallas_call(
        gradient_kernel,
        out_shape=jax.ShapeDtypeStruct((enc_dev, model), f32),
        in_specs=[VMEM] * (2 + pipes),
        out_specs=VMEM,
        compiler_params=params,
    )(key_weight.T, value_weight.T, *sums)
    returned = lax.all_to_all(
        part.reshape(pipes * experts, cap, model),
        EVERYONE,
        split_axis=0,
        concat_axis=0,
        tiled=True,
    ).reshape(pipes, experts * cap, model)
    layer_out = pl.pallas_call(
        combine_kernel,
        out_shape=jax.ShapeDtypeStruct((tok_dev, model), bf16),
        in_specs=[VMEM] * 3,
        out_specs=VMEM,
        compiler_params=params,
    )(returned, target, hidden_state)
    for level in range(experts.bit_length() - 1):
        enc_part = enc_part + crossed(enc_part, 1 << level)
    enc_grad = enc_part.astype(bf16)
    return (layer_out, enc_grad)


def solution(mesh):
    placed = (
        P("pipe", None),
        P(None, "expert"),
        P(None, "expert"),
        P("pipe", "expert"),
        P("pipe"),
        P("pipe", "expert"),
        P(("pipe", "expert"), None),
        P(),
        P(("pipe", "expert"), None),
        P("expert", None, "pipe"),
        P("expert", "pipe", None),
    )
    return jax.shard_map(
        per_device,
        mesh=mesh,
        in_specs=placed,
        out_specs=(P(("pipe", "expert"), None), P("pipe", None)),
        check_vma=False,
    )
```
